256 devices in a mesh: store: 32 (over x, z), tp: 8 (over y, core).
Axes of the slice: x: 4, y: 4, z: 8, core: 2. Of those that a mesh axis runs over, the one named last changes fastest.
Arguments:
- kv_store: bfloat16 [96, 2, 256, 1024], P('store', None, None, 'tp'), may hold values from -6 to 6
- kv_scale: bfloat16 [96, 2, 8, 2], P('store', None, 'tp'), may hold values from 0.25 to 40
- span_home: int32 [96], replicated, may hold values from 0 to 95, as said below
- doc_ids: int32 [32, 20], P('store'), may hold values from 0 to 95, as said below
- doc_count: int32 [32], P('store'), may hold values from 6 to 20, as said below
- recompute_rows: int32 [32, 4, 128], P('store'), may hold values from 0 to 5119, as said below
- query_len: int32 [32], P('store'), may hold values from 1 to 256, as said below
- hidden: bfloat16 [32, 768, 4096], P('store', None, 'tp'), may hold values from -400 to 400
- norm_gain: bfloat16 [4096], replicated, may hold values from 0.5 to 1.5
- w_q: bfloat16 [4096, 4096], P(None, 'tp'), may hold values from -0.09375 to 0.09375
- w_kv: bfloat16 [4096, 2, 1024], P(None, None, 'tp'), may hold values from -0.09375 to 0.09375
Outputs:
- attn_out: bfloat16 [32, 256, 4096], P('store', None, 'tp')
- context_kv: bfloat16 [32, 2, 5120, 1024], P('store', None, None, 'tp')
The draws below stay inside these ranges and needn't reach their ends.
Inputs may be any that keep to these rules, and one draw needn't show every extreme that they name: `span_home`: each storage position occurs once; position p lies on index p // 3 of store. `doc_ids`: the 20 ids of a request are distinct; the first doc_count are its documents; a request's ids name at most 2 spans stored on one index of store, and exactly 2 on some index. `doc_count`: some request has 20 documents. `recompute_rows`: distinct within a request and below doc_count * 256. `query_len`: some request has 256 query tokens.
All inputs are finite; a program needn't handle non-finite values.
Results may differ from the reference program's by a relative error of at most 0.015.
The reference program's roundings to bfloat16 on the way (of `cached`, `normed` and `weights`) count: a program that leaves them out, or rounds other values in their place, can miss the bound.
Values may be sent and summed in bfloat16 or wider, within the bound.
No kernel may reach another device: no remote copies, remote signals or barrier semaphores. Data moves between devices by JAX's collectives and lax.ppermute only.
A program may use at most 128 MiB of HBM per device.

```python
import math
import jax
import jax.numpy as jnp
from jax import lax

D = 4096
HD = 128
QH_DEV = 4
KVH = 8
QHEADS = 32
SPAN = 256
SB = 128
NB = 2
MAXDOC = 20
MINDOC = 6
CH_DEV = 3
SPANS = 96
CAP = 2
RB = 4
RBROWS = 128
QLEN = 256
ROWS = 768
CTXMAX = 5120
REQUESTS = 32
N_STORE = 32


def placement_order(key):
    key = jax.random.fold_in(key, 100)
    return jax.random.permutation(key, SPANS).astype(jnp.int32)


def request_counts(key):
    key = jax.random.fold_in(key, 101)
    key_one, key_two = jax.random.split(key)
    counts = jax.random.randint(key_one, (REQUESTS,), MINDOC, MAXDOC + 1)
    fullest = jax.random.randint(key_two, (), 0, REQUESTS)
    return jnp.where(jnp.arange(REQUESTS) == fullest, MAXDOC, counts).astype(jnp.int32)


def draw_span_home(key, part):
    order = placement_order(key)
    return order


def draw_doc_count(key, part):
    counts = request_counts(key)
    return counts


def draw_doc_ids(key, part):
    order = placement_order(key)
    counts = request_counts(key)
    key = jax.random.fold_in(key, 5)
    key_one, key_two, key_three, key_four = jax.random.split(key, 4)
    entries = N_STORE * CAP
    owner_dev = jnp.arange(entries) // CAP
    copy_rank = jnp.arange(entries) % CAP
    weights = jax.random.randint(key_one, (N_STORE,), 1, 9)
    raw_bits = jax.random.randint(key_two, (REQUESTS, entries), 0, 2 ** 20)
    scores = raw_bits // weights[owner_dev][None, :] * 256 + jnp.arange(entries)[None, :]
    leader = owner_dev[jnp.argmin(scores, axis=1)]
    scores = jnp.where(owner_dev[None, :] == leader[:, None], copy_rank[None, :] - CAP, scores)
    ranked = jnp.argsort(scores, axis=1)[:, :MAXDOC]
    shuffle_bits = jax.random.randint(key_three, (REQUESTS, MAXDOC), 0, 2 ** 20) * 64 + jnp.arange(MAXDOC)[None, :]
    live_slots = jnp.arange(MAXDOC)[None, :] < counts[:, None]
    shuffle_bits = jnp.where(live_slots, shuffle_bits, 2 ** 27 + jnp.arange(MAXDOC)[None, :])
    chosen = jnp.take_along_axis(ranked, jnp.argsort(shuffle_bits, axis=1), axis=1)
    chosen_dev = owner_dev[chosen]
    chosen_copy = copy_rank[chosen]
    base_slot = jax.random.randint(key_four, (REQUESTS, N_STORE), 0, CH_DEV)
    slot_index = (jnp.take_along_axis(base_slot, chosen_dev, axis=1) + chosen_copy) % CH_DEV
    storage_pos = chosen_dev * CH_DEV + slot_index
    inverse = jnp.argsort(order)
    return inverse[storage_pos].astype(jnp.int32)


def draw_recompute_rows(key, part):
    counts = request_counts(key)
    key = jax.random.fold_in(key, 7)
    raw_bits = jax.random.randint(key, (REQUESTS, CTXMAX), 0, 2 ** 17)
    scores = raw_bits * 8192 + jnp.arange(CTXMAX)[None, :]
    live_rows = jnp.arange(CTXMAX)[None, :] < counts[:, None] * SPAN
    scores = jnp.where(live_rows, scores, 2 ** 30 + jnp.arange(CTXMAX)[None, :])
    picked = jnp.argsort(scores, axis=1)[:, :RB * RBROWS]
    return picked.reshape(REQUESTS, RB, RBROWS).astype(jnp.int32)


def draw_query_len(key, part):
    key = jax.random.fold_in(key, 9)
    key_one, key_two = jax.random.split(key)
    lengths = jax.random.randint(key_one, (REQUESTS,), 1, QLEN + 1)
    fullest = jax.random.randint(key_two, (), 0, REQUESTS)
    return jnp.where(jnp.arange(REQUESTS) == fullest, QLEN, lengths).astype(jnp.int32)


def draw_kv_scale(key, part):
    key = jax.random.fold_in(key, 11)
    key_one = jax.random.fold_in(key, 0)
    shape_all = (SPANS, 2, KVH, NB)
    scales = jnp.exp(jax.random.uniform(key_one, shape_all, jnp.float32, math.log(0.25), math.log(3.0)))
    return scales.astype(jnp.bfloat16)


def draw_hidden(key, part):
    key = jax.random.fold_in(key, 13)
    key_one, key_two, key_three = jax.random.split(key, 3)
    shape_all = (REQUESTS, ROWS, D)
    row_scale = jnp.exp(jax.random.uniform(key_one, (REQUESTS, ROWS, 1), jnp.float32, 0.0, math.log(10.0)))
    column_scale = jnp.exp(jax.random.uniform(key_two, (1, 1, D), jnp.float32, 0.0, math.log(10.0)))
    values = jnp.clip(jax.random.normal(key_three, shape_all, jnp.float32), -4.0, 4.0)
    return (values * row_scale * column_scale).astype(jnp.bfloat16)


def block_scale(stream_key, shape, shards, low, largest):
    loudness, own = 1.0, jax.random.fold_in(stream_key, 6)
    for dim, blocks in shards:
        steps = jnp.exp(jax.random.uniform(jax.random.fold_in(own, dim), (blocks,), jnp.float32, low / len(shards), largest / len(shards)))
        loudness = loudness * jnp.repeat(steps, shape[dim] // blocks).reshape([-1 if axis == dim else 1 for axis in range(len(shape))])
    return loudness


def centred(own_key, extent, deviation, limit, cuts=(), held_as=jnp.bfloat16):
    result = jax.random.normal(own_key, extent, jnp.float32) * deviation
    if len(cuts) > 0:
        result = block_scale(own_key, extent, cuts, -0.22, 0.18) * result
    return jnp.clip(result, min=-limit, max=limit).astype(held_as)


def setup_inputs(seed: int = 0) -> dict:
    key_of = jax.random.split(jax.random.key(seed), 12)
    kv_store = centred(key_of[0], (SPANS, 2, SPAN, KVH * HD), 1.0, 6.0, ((0, 32), (3, 8)))
    kv_scale = draw_kv_scale(jax.random.fold_in(key_of[11], 71), 0)
    span_home = draw_span_home(jax.random.fold_in(key_of[11], 71), 0)
    doc_ids = draw_doc_ids(jax.random.fold_in(key_of[11], 71), 0)
    doc_count = draw_doc_count(jax.random.fold_in(key_of[11], 71), 0)
    recompute_rows = draw_recompute_rows(jax.random.fold_in(key_of[11], 71), 0)
    query_len = draw_query_len(jax.random.fold_in(key_of[11], 71), 0)
    hidden = draw_hidden(jax.random.fold_in(key_of[11], 71), 0)
    norm_gain = jnp.clip(1.0 + 0.1 * jax.random.normal(key_of[8], (D,), jnp.float32), 0.5, 1.5).astype(jnp.bfloat16)
    w_q = centred(key_of[9], (D, QHEADS * HD), D ** -0.5, 0.09375, ((1, 8),))
    w_kv = centred(key_of[10], (D, 2, KVH * HD), D ** -0.5, 0.09375, ((2, 8),))
    return {"kv_store": kv_store, "kv_scale": kv_scale, "span_home": span_home, "doc_ids": doc_ids, "doc_count": doc_count, "recompute_rows": recompute_rows, "query_len": query_len, "hidden": hidden, "norm_gain": norm_gain, "w_q": w_q, "w_kv": w_kv}


rope_base = 500000.0
norm_eps = 1e-05

def rope_angles(positions, head_width):
    halfway = head_width // 2
    exponent = jnp.arange(halfway, dtype=jnp.float32) * (2.0 / head_width)
    inverse_freq = jnp.power(jnp.float32(rope_base), -exponent)
    angles = positions.astype(jnp.float32)[:, None] * inverse_freq[None, :]
    return (jnp.cos(angles), jnp.sin(angles))

def rotate_half(values, cosine, sine_part):
    halfway = values.shape[-1] // 2
    low_half = values[..., :halfway]
    high_half = values[..., halfway:]
    return jnp.concatenate([low_half * cosine - high_half * sine_part, high_half * cosine + low_half * sine_part], axis=-1)

def reference(kv_store, kv_scale, span_home, doc_ids, doc_count, recompute_rows, query_len, hidden, norm_gain, w_q, w_kv):
    recompute_total = RB * RBROWS
    context_max = MAXDOC * SPAN
    kv_heads = KVH

    def one_request(request):
        doc_list, doc_total, recompute_pos, query_total, layer_input = request
        position = span_home[doc_list]
        codes = kv_store[position].astype(jnp.float32).reshape(MAXDOC, 2, SPAN, kv_heads, HD)
        scales = jnp.repeat(kv_scale[position].astype(jnp.float32), SB, axis=3)
        scales = jnp.transpose(scales, (0, 1, 3, 2))
        dequant = codes * scales[..., None]
        shift_cos, shift_sin = rope_angles(jnp.arange(MAXDOC, dtype=jnp.int32) * SPAN, HD)
        cached_keys = rotate_half(dequant[:, 0], shift_cos[:, None, None, :], shift_sin[:, None, None, :])
        cached = jnp.stack([cached_keys, dequant[:, 1]], axis=0).reshape(2, context_max, kv_heads * HD)
        live_rows = jnp.arange(context_max) < doc_total * SPAN
        cached = jnp.where(live_rows[None, :, None], cached, 0.0).astype(jnp.bfloat16)
        features = layer_input.astype(jnp.float32)
        inverse_rms = lax.rsqrt(lax.optimization_barrier(jnp.mean(features * features, axis=-1, keepdims=True)) + norm_eps)
        normed = (features * inverse_rms * norm_gain.astype(jnp.float32)).astype(jnp.bfloat16)
        query_proj = jnp.dot(normed[recompute_total:], w_q, preferred_element_type=jnp.float32)
        kv_proj = jnp.dot(normed, w_kv.reshape(D, 2 * kv_heads * HD), preferred_element_type=jnp.float32)
        kv_proj = kv_proj.reshape(-1, 2, kv_heads, HD)
        flat_pos = recompute_pos.reshape(recompute_total).astype(jnp.int32)
        query_pos = doc_total * SPAN + jnp.arange(QLEN, dtype=jnp.int32)
        row_cos, row_sin = rope_angles(jnp.concatenate([flat_pos, query_pos.astype(jnp.int32)]), HD)
        new_keys = rotate_half(kv_proj[:, 0], row_cos[:, None, :], row_sin[:, None, :]).astype(jnp.bfloat16)
        new_values = kv_proj[:, 1].astype(jnp.bfloat16)
        queries = rotate_half(query_proj.reshape(QLEN, QHEADS, HD), row_cos[recompute_total:, None, :], row_sin[recompute_total:, None, :]).astype(jnp.bfloat16)
        patched = cached.at[0, flat_pos].set(new_keys[:recompute_total].reshape(recompute_total, kv_heads * HD))
        patched = patched.at[1, flat_pos].set(new_values[:recompute_total].reshape(recompute_total, kv_heads * HD))
        all_keys = jnp.concatenate([patched[0].reshape(context_max, kv_heads, HD), new_keys[recompute_total:]], axis=0)
        all_values = jnp.concatenate([patched[1].reshape(context_max, kv_heads, HD), new_values[recompute_total:]], axis=0)
        query_index = jnp.arange(QLEN)
        key_index = jnp.arange(context_max + QLEN)
        allowed = jnp.where(key_index[None, :] < context_max, (key_index < doc_total * SPAN)[None, :], key_index[None, :] - context_max <= query_index[:, None])
        head_queries = jnp.transpose(queries.reshape(QLEN, kv_heads, QH_DEV, HD), (1, 2, 0, 3))
        head_keys = jnp.transpose(all_keys, (1, 0, 2))
        head_values = jnp.transpose(all_values, (1, 0, 2))

        def one_head(inputs):
            group_queries, group_keys, group_values = inputs
            scores = jnp.einsum('hqd,kd->hqk', group_queries.astype(jnp.float32), group_keys.astype(jnp.float32)) * HD ** (-0.5)
            scores = jnp.where(allowed[None], scores, -jnp.inf)
            top_score = lax.optimization_barrier(jnp.max(scores, axis=-1, keepdims=True))
            exp_terms = jnp.where(allowed[None], jnp.exp(scores - top_score), 0.0)
            weights = (exp_terms / lax.optimization_barrier(jnp.sum(exp_terms, axis=-1, keepdims=True))).astype(jnp.bfloat16)
            return jnp.einsum('hqk,kd->hqd', weights.astype(jnp.float32), group_values.astype(jnp.float32))
        mixed_heads = lax.map(one_head, (head_queries, head_keys, head_values))
        mixed_rows = jnp.transpose(mixed_heads, (2, 0, 1, 3)).reshape(QLEN, QHEADS * HD)
        mixed_rows = jnp.where((query_index < query_total)[:, None], mixed_rows, 0.0)
        return (mixed_rows.astype(jnp.bfloat16), patched)
    attn_out, context_kv = lax.map(one_request, (doc_ids, doc_count, recompute_rows, query_len, hidden))
    return (attn_out, context_kv)
```

```python
import functools
import jax
import jax.numpy as jnp
from jax import lax
from jax.experimental import pallas as pl
from jax.experimental.pallas import tpu as pltpu
from jax.sharding import PartitionSpec as P

SPAN = 256
SB = 128
MAXDOC = 20
NX, NZ = 4, 8
HW = 128
LOG2E = 1.4426950408889634


rope_base = 500000.0
norm_eps = 1e-05


def rope_angles(positions, head_width):
    halfway = head_width // 2
    exponent = jnp.arange(halfway, dtype=jnp.float32) * (2.0 / head_width)
    inverse_freq = jnp.power(jnp.float32(rope_base), -exponent)
    angles = positions.astype(jnp.float32)[:, None] * inverse_freq[None, :]
    return (jnp.cos(angles), jnp.sin(angles))


def rotate_half(values, cosine, sine_part):
    halfway = values.shape[-1] // 2
    low_half = values[..., :halfway]
    high_half = values[..., halfway:]
    return jnp.concatenate(
        [low_half * cosine - high_half * sine_part, high_half * cosine + low_half * sine_part],
        axis=-1,
    )


def shift(a, dx, dz):
    pairs = [
        (x * NZ + z, ((x + dx) % NX) * NZ + (z + dz) % NZ) for x in range(NX) for z in range(NZ)
    ]
    return lax.ppermute(a, "store", pairs)


def ring_x(own, cut):
    a, b = shift(own, 1, 0), shift(own, -1, 0)
    return [own, a, b, shift(a[:cut], 1, 0), shift(b[cut:], -1, 0)]


def ring_z(own, cut):
    out, p, q = [own], own, own
    for _ in range(3):
        p, q = shift(p, 0, 1), shift(q, 0, -1)
        out += [p, q]
    return out + [shift(p[:cut], 0, 1), shift(q[cut:], 0, -1)]


def attend_kernel(
    nk,
    nv,
    where_ref,
    scale_ref,
    count_ref,
    pos_ref,
    shift_ref,
    new_ref,
    qt_ref,
    *refs,
):
    kbufs, vbufs = refs[:nk], refs[nk : nk + nv]
    out_ref, ctx_ref = refs[nk + nv : nk + nv + 2]
    kdoc, vdoc, m_ref, l_ref, acc_ref, ksem, vsem, kout, vout = refs[nk + nv + 2 :]
    docs = count_ref[0]
    qlen = count_ref[1]
    lanes = qt_ref.shape[1]
    nrec = pos_ref.shape[1]
    factor = HW**-0.5 * LOG2E

    def fetch(j, _):
        for b in range(nk):

            @pl.when(where_ref[0, j] == b)
            def _():
                pltpu.make_async_copy(
                    kbufs[b].at[where_ref[1, j]], kdoc.at[j], ksem.at[j]
                ).start()

        for b in range(nv):

            @pl.when(where_ref[2, j] == b)
            def _():
                pltpu.make_async_copy(
                    vbufs[b].at[where_ref[3, j]], vdoc.at[j], vsem.at[j]
                ).start()

        return 0

    lax.fori_loop(0, docs, fetch, 0)

    def store(j):
        pltpu.make_async_copy(kdoc.at[j], ctx_ref.at[0, pl.ds(j * SPAN, SPAN)], kout.at[j]).start()
        pltpu.make_async_copy(vdoc.at[j], ctx_ref.at[1, pl.ds(j * SPAN, SPAN)], vout.at[j]).start()

    def blank(j, _):
        kdoc[j] = jnp.zeros((SPAN, HW), jnp.bfloat16)
        vdoc[j] = jnp.zeros((SPAN, HW), jnp.bfloat16)
        store(j)
        return 0

    lax.fori_loop(docs, MAXDOC, blank, 0)

    own_keys = new_ref[nrec:, :HW]
    own_values = new_ref[nrec:, HW : 2 * HW]
    scores = jnp.dot(own_keys, qt_ref[...], preferred_element_type=jnp.float32)
    key_index = lax.broadcasted_iota(jnp.int32, scores.shape, 0)
    query_index = lax.broadcasted_iota(jnp.int32, scores.shape, 1) & (SPAN - 1)
    allowed = key_index <= query_index
    scores = jnp.where(allowed, scores, -jnp.inf)
    top = jnp.max(scores, axis=0, keepdims=True)
    terms = jnp.exp2((scores - top) * factor)
    m_ref[...] = top
    l_ref[...] = jnp.sum(terms, axis=0, keepdims=True)
    acc_ref[...] = lax.dot_general(
        own_values,
        terms.astype(jnp.bfloat16),
        (((0,), (0,)), ((), ())),
        preferred_element_type=jnp.float32,
    )
    high = lax.broadcasted_iota(jnp.int32, (SPAN, HW), 0) >= SB
    row_index = lax.broadcasted_iota(jnp.int32, (SPAN, nrec), 0)

    def step(j, _):
        pltpu.make_async_copy(kbufs[0].at[0], kdoc.at[j], ksem.at[j]).wait()
        pltpu.make_async_copy(vbufs[0].at[0], vdoc.at[j], vsem.at[j]).wait()
        hit = jnp.where(row_index == pos_ref[...] - j * SPAN, 1.0, 0.0).astype(jnp.bfloat16)
        fresh = jnp.dot(hit, new_ref[:nrec], preferred_element_type=jnp.float32)
        replaced = fresh[:, 2 * HW :] > 0.5
        k = kdoc[j].astype(jnp.float32) * jnp.where(high, scale_ref[4 * j + 1], scale_ref[4 * j])
        turn = shift_ref[j]
        k = k * turn[0:1] + pltpu.roll(k, HW // 2, 1) * turn[1:2]
        k = jnp.where(replaced, fresh[:, :HW], k).astype(jnp.bfloat16)
        v = vdoc[j].astype(jnp.float32) * jnp.where(
            high, scale_ref[4 * j + 3], scale_ref[4 * j + 2]
        )
        v = jnp.where(replaced, fresh[:, HW : 2 * HW], v).astype(jnp.bfloat16)
        kdoc[j] = k
        vdoc[j] = v
        store(j)
        scores = jnp.dot(k, qt_ref[...], preferred_element_type=jnp.float32)
        before = m_ref[...]
        top = jnp.maximum(before, jnp.max(scores, axis=0, keepdims=True))
        terms = jnp.exp2((scores - top) * factor)
        fade = jnp.exp2((before - top) * factor)
        m_ref[...] = top
        l_ref[...] = l_ref[...] * fade + jnp.sum(terms, axis=0, keepdims=True)
        acc_ref[...] = acc_ref[...] * fade + lax.dot_general(
            v,
            terms.astype(jnp.bfloat16),
            (((0,), (0,)), ((), ())),
            preferred_element_type=jnp.float32,
        )
        return 0

    lax.fori_loop(0, docs, step, 0)

    live = (lax.broadcasted_iota(jnp.int32, (1, lanes), 1) & (SPAN - 1)) < qlen
    mixed = jnp.where(live, acc_ref[...] / l_ref[...], 0.0)
    for h in range(lanes // SPAN):
        out_ref[:, h * HW : (h + 1) * HW] = mixed[:, h * SPAN : (h + 1) * SPAN].T.astype(
            jnp.bfloat16
        )

    def finish(j, _):
        pltpu.make_async_copy(kdoc.at[j], ctx_ref.at[0, pl.ds(j * SPAN, SPAN)], kout.at[j]).wait()
        pltpu.make_async_copy(vdoc.at[j], ctx_ref.at[1, pl.ds(j * SPAN, SPAN)], vout.at[j]).wait()
        return 0

    lax.fori_loop(0, MAXDOC, finish, 0)


def attend(kbufs, vbufs, where, scales, counts, pos, turns, new, qt):
    lanes = qt.shape[1]
    smem = pl.BlockSpec(memory_space=pltpu.SMEM)
    vmem = pl.BlockSpec(memory_space=pltpu.VMEM)
    hbm = pl.BlockSpec(memory_space=pl.ANY)
    return pl.pallas_call(
        functools.partial(attend_kernel, len(kbufs), len(vbufs)),
        out_shape=(
            jax.ShapeDtypeStruct((SPAN, lanes // SPAN * HW), jnp.bfloat16),
            jax.ShapeDtypeStruct((2, MAXDOC * SPAN, HW), jnp.bfloat16),
        ),
        in_specs=[smem] * 3 + [vmem] * 4 + [hbm] * (len(kbufs) + len(vbufs)),
        out_specs=(vmem, hbm),
        scratch_shapes=[
            pltpu.VMEM((MAXDOC, SPAN, HW), jnp.bfloat16),
            pltpu.VMEM((MAXDOC, SPAN, HW), jnp.bfloat16),
            pltpu.VMEM((1, lanes), jnp.float32),
            pltpu.VMEM((1, lanes), jnp.float32),
            pltpu.VMEM((HW, lanes), jnp.float32),
            pltpu.SemaphoreType.DMA((MAXDOC,)),
            pltpu.SemaphoreType.DMA((MAXDOC,)),
            pltpu.SemaphoreType.DMA((MAXDOC,)),
            pltpu.SemaphoreType.DMA((MAXDOC,)),
        ],
        compiler_params=pltpu.CompilerParams(vmem_limit_bytes=32 * 1024 * 1024),
        cost_estimate=pl.CostEstimate(
            flops=4 * lanes * HW * (MAXDOC + 1) * SPAN,
            bytes_accessed=8 * MAXDOC * SPAN * HW,
            transcendentals=lanes * (MAXDOC + 1) * SPAN,
        ),
    )(where, scales, counts, pos, turns, new, qt, *kbufs, *vbufs)


def on_device(
    kv_store,
    kv_scale,
    span_home,
    doc_ids,
    doc_count,
    recompute_rows,
    query_len,
    hidden,
    norm_gain,
    w_q,
    w_kv,
):
    peers = lax.axis_size("store")
    stored = kv_store.shape[0]
    me = lax.axis_index("store")
    my_x, my_z = me // NZ, me % NZ

    keys, values = kv_store[:, 0], kv_store[:, 1]
    v12 = jnp.concatenate(ring_x(values, 2), axis=0)
    k24 = jnp.concatenate(ring_z(keys, 2), axis=0)
    kbufs = ring_x(k24, NZ * stored // 2)
    vbufs = ring_z(v12, NX * stored // 2)
    flat_scale = kv_scale.reshape(1, -1)
    all_scales = lax.all_to_all(
        jnp.broadcast_to(flat_scale, (peers, flat_scale.shape[1])),
        "store",
        split_axis=0,
        concat_axis=0,
        tiled=True,
    ).reshape(peers * stored, -1)

    doc_list = doc_ids[0]
    doc_total = doc_count[0]
    span_index = jnp.arange(span_home.shape[0], dtype=jnp.int32)
    position = jnp.sum(
        jnp.where(doc_list[:, None] == span_index[None, :], span_home[None, :], 0), axis=1
    )
    owner, slot = position // stored, position % stored
    dx = (owner // NZ - my_x) % NX
    dz = (owner % NZ - my_z) % NZ
    rank_x = jnp.where(dx == 0, 0, jnp.where(dx == 3, 1, jnp.where(dx == 1, 2, 3)))
    rank_z = jnp.where(dz == 4, 7, jnp.where(dz == 0, 0, jnp.where(dz > 4, 15 - 2 * dz, 2 * dz)))
    k_at = rank_z * stored + slot
    v_at = rank_x * stored + slot
    half_k, half_v = NZ * stored // 2, NX * stored // 2
    k_split = (rank_x == 3) & (k_at >= half_k)
    v_split = (rank_z == 7) & (v_at >= half_v)
    where = jnp.stack(
        [
            rank_x + k_split.astype(jnp.int32),
            k_at - jnp.where(k_split, half_k, 0),
            rank_z + v_split.astype(jnp.int32),
            v_at - jnp.where(v_split, half_v, 0),
        ]
    ).astype(jnp.int32)
    home = position[:, None] == jnp.arange(peers * stored)[None, :]
    scales = jnp.sum(
        jnp.where(home[:, :, None], all_scales.astype(jnp.float32)[None], 0.0), axis=1
    ).reshape(-1)

    shift_cos, shift_sin = rope_angles(jnp.arange(MAXDOC, dtype=jnp.int32) * SPAN, HW)
    turns = jnp.stack(
        [
            jnp.concatenate([shift_cos, shift_cos], axis=1),
            jnp.concatenate([-shift_sin, shift_sin], axis=1),
        ],
        axis=1,
    )

    layer_input = lax.all_gather(hidden, "tp", axis=2, tiled=True)[0]
    features = layer_input.astype(jnp.float32)
    inverse_rms = lax.rsqrt(jnp.mean(features * features, axis=-1, keepdims=True) + norm_eps)
    normed = (features * inverse_rms * norm_gain.astype(jnp.float32)).astype(jnp.bfloat16)
    recompute_total = recompute_rows.shape[1] * recompute_rows.shape[2]
    query_rows = layer_input.shape[0] - recompute_total
    query_heads = w_q.shape[1] // HW
    query_proj = jnp.dot(normed[recompute_total:], w_q, preferred_element_type=jnp.float32)
    kv_proj = jnp.dot(
        normed, w_kv.reshape(w_kv.shape[0], 2 * HW), preferred_element_type=jnp.float32
    )
    kv_proj = kv_proj.reshape(-1, 2, HW)
    flat_pos = recompute_rows[0].reshape(recompute_total)
    query_pos = doc_total * SPAN + jnp.arange(query_rows, dtype=jnp.int32)
    row_cos, row_sin = rope_angles(jnp.concatenate([flat_pos, query_pos]), HW)
    new_keys = rotate_half(kv_proj[:, 0], row_cos, row_sin).astype(jnp.bfloat16)
    new_values = kv_proj[:, 1].astype(jnp.bfloat16)
    queries = rotate_half(
        query_proj.reshape(query_rows, query_heads, HW),
        row_cos[recompute_total:, None, :],
        row_sin[recompute_total:, None, :],
    ).astype(jnp.bfloat16)
    qt = jnp.transpose(queries, (2, 1, 0)).reshape(HW, query_heads * query_rows)
    new = jnp.concatenate([new_keys, new_values, jnp.ones_like(new_keys)], axis=1)

    attention, context = attend(
        kbufs,
        vbufs,
        where,
        scales,
        jnp.stack([doc_total, query_len[0]]).astype(jnp.int32),
        flat_pos.astype(jnp.int32)[None],
        turns,
        new,
        qt,
    )
    return (attention[None], context[None])


def solution(mesh):
    placed = (
        P("store", None, None, "tp"),
        P("store", None, "tp", None),
        P(),
        P("store", None),
        P("store"),
        P("store", None, None),
        P("store"),
        P("store", None, "tp"),
        P(),
        P(None, "tp"),
        P(None, None, "tp"),
    )
    return jax.shard_map(
        on_device,
        mesh=mesh,
        in_specs=placed,
        out_specs=(P("store", None, "tp"), P("store", None, None, "tp")),
        check_vma=False,
    )
```

```python
import functools
import jax
import jax.numpy as jnp
from jax import lax
from jax.experimental import pallas as pl
from jax.experimental.pallas import tpu as pltpu
from jax.sharding import PartitionSpec as P

SPAN = 256
SB = 128
MAXDOC = 20
NX, NZ = 4, 8
HW = 128
LOG2E = 1.4426950408889634
STORED = 3
BLOCK = STORED * SPAN + 16
CUT = BLOCK + 2 * SPAN


rope_base = 500000.0
norm_eps = 1e-05


def rope_angles(positions, head_width):
    halfway = head_width // 2
    exponent = jnp.arange(halfway, dtype=jnp.float32) * (2.0 / head_width)
    inverse_freq = jnp.power(jnp.float32(rope_base), -exponent)
    angles = positions.astype(jnp.float32)[:, None] * inverse_freq[None, :]
    return (jnp.cos(angles), jnp.sin(angles))


def rotate_half(values, cosine, sine_part):
    halfway = values.shape[-1] // 2
    low_half = values[..., :halfway]
    high_half = values[..., halfway:]
    return jnp.concatenate(
        [low_half * cosine - high_half * sine_part, high_half * cosine + low_half * sine_part],
        axis=-1,
    )


def shift(a, dx, dz):
    pairs = [
        (x * NZ + z, ((x + dx) % NX) * NZ + (z + dz) % NZ) for x in range(NX) for z in range(NZ)
    ]
    return lax.ppermute(a, "store", pairs)


HBM = pl.BlockSpec(memory_space=pl.ANY)
VMEM = pl.BlockSpec(memory_space=pltpu.VMEM)
SMEM = pl.BlockSpec(memory_space=pltpu.SMEM)


def pack_kernel(plan, *refs):
    sources, out, sems = refs[:-2], refs[-2], refs[-1]
    copies, at = [], 0
    for n, (source, start, rows) in enumerate(plan):
        copies.append(
            pltpu.make_async_copy(
                sources[source].at[pl.ds(start, rows)], out.at[pl.ds(at, rows)], sems.at[n]
            )
        )
        at += rows
    for copy in copies:
        copy.start()
    for copy in copies:
        copy.wait()


def pack(sources, plan):
    rows = sum(p[2] for p in plan)
    return pl.pallas_call(
        functools.partial(pack_kernel, plan),
        out_shape=jax.ShapeDtypeStruct((rows, HW), jnp.bfloat16),
        in_specs=[HBM] * len(sources),
        out_specs=HBM,
        scratch_shapes=[pltpu.SemaphoreType.DMA((len(plan),))],
        cost_estimate=pl.CostEstimate(
            flops=0, bytes_accessed=4 * rows * HW, transcendentals=0
        ),
    )(*sources)


def project_kernel(hid_ref, gain_ref, wq_ref, wkv_ref, cos_ref, sin_ref, new_ref, qt_ref, nb_ref):
    features = hid_ref.shape[1]
    piece = 512
    total = jnp.zeros((SPAN, 1), jnp.float32)
    for c in range(0, features, piece):
        x = hid_ref[:, c : c + piece].astype(jnp.float32)
        total = total + jnp.sum(x * x, axis=1, keepdims=True)
    inverse = lax.rsqrt(total * (1.0 / features) + norm_eps)
    for c in range(0, features, piece):
        x = hid_ref[:, c : c + piece].astype(jnp.float32)
        gain = gain_ref[:, c : c + piece].astype(jnp.float32)
        nb_ref[:, c : c + piece] = (x * inverse * gain).astype(jnp.bfloat16)
    kv = jnp.dot(nb_ref[...], wkv_ref[...], preferred_element_type=jnp.float32)
    cosine, sine = cos_ref[...], sin_ref[...]
    k = kv[:, :HW]
    new_ref[:, :HW] = (k * cosine + pltpu.roll(k, HW // 2, 1) * sine).astype(jnp.bfloat16)
    new_ref[:, HW : 2 * HW] = kv[:, HW:].astype(jnp.bfloat16)
    new_ref[:, 2 * HW :] = jnp.ones((SPAN, HW), jnp.bfloat16)

    @pl.when(pl.program_id(0) == pl.num_programs(0) - 1)
    def _():
        q = jnp.dot(nb_ref[...], wq_ref[...], preferred_element_type=jnp.float32)
        for h in range(q.shape[1] // HW):
            one = q[:, h * HW : (h + 1) * HW]
            one = one * cosine + pltpu.roll(one, HW // 2, 1) * sine
            qt_ref[:, h * SPAN : (h + 1) * SPAN] = one.T.astype(jnp.bfloat16)


def project(hid, gain, wq, wkv, cosine, sine):
    rows, features = hid.shape
    lanes = wq.shape[1] // HW * SPAN
    return pl.pallas_call(
        project_kernel,
        grid=(rows // SPAN,),
        out_shape=(
            jax.ShapeDtypeStruct((rows, 3 * HW), jnp.bfloat16),
            jax.ShapeDtypeStruct((HW, lanes), jnp.bfloat16),
        ),
        in_specs=[
            pl.BlockSpec((SPAN, features), lambda i: (i, 0)),
            pl.BlockSpec((1, features), lambda i: (0, 0)),
            pl.BlockSpec(wq.shape, lambda i: (0, 0)),
            pl.BlockSpec(wkv.shape, lambda i: (0, 0)),
            pl.BlockSpec((SPAN, HW), lambda i: (i, 0)),
            pl.BlockSpec((SPAN, HW), lambda i: (i, 0)),
        ],
        out_specs=(
            pl.BlockSpec((SPAN, 3 * HW), lambda i: (i, 0)),
            pl.BlockSpec((HW, lanes), lambda i: (0, 0)),
        ),
        scratch_shapes=[pltpu.VMEM((SPAN, features), jnp.bfloat16)],
        compiler_params=pltpu.CompilerParams(vmem_limit_bytes=40 * 1024 * 1024),
        cost_estimate=pl.CostEstimate(
            flops=2 * features * HW * (2 * rows + 4 * SPAN),
            bytes_accessed=2 * features * (rows + 6 * HW),
            transcendentals=0,
        ),
    )(hid, gain, wq, wkv, cosine, sine)


DOC, SLOT, KB, KROW, KSC, VB, VROW, VSC = range(8)


def attend_kernel(first, nk, nv, table, count_ref, pos_ref, shift_ref, new_ref, qt_ref, *refs):
    kbufs, vbufs, refs = refs[:nk], refs[nk : nk + nv], refs[nk + nv :]
    if first:
        ctx_ref, m_ref, l_ref, acc_ref = refs[:4]
        refs = refs[4:]
    else:
        m_in, l_in, acc_in, _, out_ref, ctx_ref, m_ref, l_ref, acc_ref = refs[:9]
        refs = refs[9:]
    kdoc, vdoc, kscale, vscale, zero, ksem, vsem, kssem, vssem, kout, vout = refs
    count = count_ref[2] if first else count_ref[3]
    lanes = qt_ref.shape[1]
    nrec = pos_ref.shape[1]
    factor = HW**-0.5 * LOG2E
    heads = [slice(h, h + SPAN) for h in range(0, lanes, SPAN)]

    def pick(n, low, high, act):
        if high - low == 1:
            act(low)
            return
        mid = (low + high) // 2

        @pl.when(n < mid)
        def _():
            pick(n, low, mid, act)

        @pl.when(n >= mid)
        def _():
            pick(n, mid, high, act)

    def fetch(r, _):
        def keys(b):
            row = pl.multiple_of(table[KROW, r], 16)
            pltpu.make_async_copy(kbufs[b].at[pl.ds(row, SPAN)], kdoc.at[r], ksem.at[r]).start()
            row = pl.multiple_of(table[KSC, r], 16)
            pltpu.make_async_copy(kbufs[b].at[pl.ds(row, 16)], kscale.at[r], kssem.at[r]).start()

        def values(b):
            row = pl.multiple_of(table[VROW, r], 16)
            pltpu.make_async_copy(vbufs[b].at[pl.ds(row, SPAN)], vdoc.at[r], vsem.at[r]).start()
            row = pl.multiple_of(table[VSC, r], 16)
            pltpu.make_async_copy(vbufs[b].at[pl.ds(row, 16)], vscale.at[r], vssem.at[r]).start()

        pick(table[KB, r], 0, nk, keys)
        pick(table[VB, r], 0, nv, values)
        return 0

    lax.fori_loop(0, count, fetch, 0)

    def place(j):
        return pl.ds(pl.multiple_of(j * SPAN, SPAN), SPAN)

    if first:
        docs = count_ref[0]
        zero[...] = jnp.zeros(zero.shape, zero.dtype)

        def blank(j, _):
            pltpu.make_async_copy(zero, ctx_ref.at[0, place(j)], kout.at[j]).start()
            pltpu.make_async_copy(zero, ctx_ref.at[1, place(j)], vout.at[j]).start()
            return 0

        lax.fori_loop(docs, MAXDOC, blank, 0)

        own_keys = new_ref[nrec:, :HW]
        own_values = new_ref[nrec:, HW : 2 * HW]
        for h in heads:
            scores = jnp.dot(own_keys, qt_ref[:, h], preferred_element_type=jnp.float32)
            key_index = lax.broadcasted_iota(jnp.int32, scores.shape, 0)
            query_index = lax.broadcasted_iota(jnp.int32, scores.shape, 1)
            scores = jnp.where(key_index <= query_index, scores, -jnp.inf)
            top = jnp.max(scores, axis=0, keepdims=True)
            terms = jnp.exp2((scores - top) * factor)
            m_ref[:, h] = top
            l_ref[:, h] = jnp.sum(terms, axis=0, keepdims=True)
            acc_ref[:, h] = lax.dot_general(
                own_values,
                terms.astype(jnp.bfloat16),
                (((0,), (0,)), ((), ())),
                preferred_element_type=jnp.float32,
            )
    else:
        m_ref[...] = m_in[...]
        l_ref[...] = l_in[...]
        acc_ref[...] = acc_in[...]

    upper = lax.broadcasted_iota(jnp.int32, (SPAN, HW), 0) >= SB
    row_index = lax.broadcasted_iota(jnp.int32, (SPAN, nrec), 0)
    scale_index = lax.broadcasted_iota(jnp.int32, (16, HW), 0)

    def dequant(codes, scales, slot):
        s = scales.astype(jnp.float32)
        low = jnp.sum(jnp.where(scale_index == 2 * slot, s, 0.0), axis=0, keepdims=True)
        high = jnp.sum(jnp.where(scale_index == 2 * slot + 1, s, 0.0), axis=0, keepdims=True)
        return codes.astype(jnp.float32) * jnp.where(upper, high, low)

    def step(r, _):
        j, slot = table[DOC, r], table[SLOT, r]
        hit = jnp.where(row_index == pos_ref[...] - j * SPAN, 1.0, 0.0).astype(jnp.bfloat16)
        fresh = jnp.dot(hit, new_ref[:nrec], preferred_element_type=jnp.float32)
        replaced = fresh[:, 2 * HW :] > 0.5
        pltpu.make_async_copy(kbufs[0].at[pl.ds(0, SPAN)], kdoc.at[r], ksem.at[r]).wait()
        pltpu.make_async_copy(kbufs[0].at[pl.ds(0, 16)], kscale.at[r], kssem.at[r]).wait()
        pltpu.make_async_copy(vbufs[0].at[pl.ds(0, SPAN)], vdoc.at[r], vsem.at[r]).wait()
        pltpu.make_async_copy(vbufs[0].at[pl.ds(0, 16)], vscale.at[r], vssem.at[r]).wait()
        k = dequant(kdoc[r], kscale[r], slot)
        turn = shift_ref[j]
        k = k * turn[0:1] + pltpu.roll(k, HW // 2, 1) * turn[1:2]
        k = jnp.where(replaced, fresh[:, :HW], k).astype(jnp.bfloat16)
        v = dequant(vdoc[r], vscale[r], slot)
        v = jnp.where(replaced, fresh[:, HW : 2 * HW], v).astype(jnp.bfloat16)
        kdoc[r] = k
        vdoc[r] = v
        pltpu.make_async_copy(kdoc.at[r], ctx_ref.at[0, place(j)], kout.at[r]).start()
        pltpu.make_async_copy(vdoc.at[r], ctx_ref.at[1, place(j)], vout.at[r]).start()
        for h in heads:
            scores = jnp.dot(k, qt_ref[:, h], preferred_element_type=jnp.float32)
            before = m_ref[:, h]
            top = jnp.maximum(before, jnp.max(scores, axis=0, keepdims=True))
            terms = jnp.exp2((scores - top) * factor)
            fade = jnp.exp2((before - top) * factor)
            m_ref[:, h] = top
            l_ref[:, h] = l_ref[:, h] * fade + jnp.sum(terms, axis=0, keepdims=True)
            acc_ref[:, h] = acc_ref[:, h] * fade + lax.dot_general(
                v,
                terms.astype(jnp.bfloat16),
                (((0,), (0,)), ((), ())),
                preferred_element_type=jnp.float32,
            )
        return 0

    lax.fori_loop(0, count, step, 0)

    if not first:
        live = lax.broadcasted_iota(jnp.int32, (1, SPAN), 1) < count_ref[1]
        for n, h in enumerate(heads):
            mixed = jnp.where(live, acc_ref[:, h] / l_ref[:, h], 0.0)
            out_ref[:, n * HW : (n + 1) * HW] = mixed.T.astype(jnp.bfloat16)

    def finish(r, _):
        pltpu.make_async_copy(kdoc.at[0], ctx_ref.at[0, pl.ds(0, SPAN)], kout.at[r]).wait()
        pltpu.make_async_copy(vdoc.at[0], ctx_ref.at[1, pl.ds(0, SPAN)], vout.at[r]).wait()
        return 0

    lax.fori_loop(0, count, finish, 0)
    if first:
        lax.fori_loop(count_ref[0], MAXDOC, finish, 0)


def attend(first, kbufs, vbufs, table, counts, pos, turns, new, qt, state):
    lanes = qt.shape[1]
    context = jax.ShapeDtypeStruct((2, MAXDOC * SPAN, HW), jnp.bfloat16)
    running = [(1, lanes), (1, lanes), (HW, lanes)]
    if first:
        out_shape = (context, *[jax.ShapeDtypeStruct(s, jnp.float32) for s in running])
        out_specs = (HBM, VMEM, VMEM, VMEM)
    else:
        out_shape = (jax.ShapeDtypeStruct((SPAN, lanes // SPAN * HW), jnp.bfloat16), context)
        out_specs = (VMEM, HBM)
    fixed = 6 + len(kbufs) + len(vbufs)
    documents = MAXDOC // 2
    return pl.pallas_call(
        functools.partial(attend_kernel, first, len(kbufs), len(vbufs)),
        out_shape=out_shape,
        in_specs=[SMEM] * 2
        + [VMEM] * 4
        + [HBM] * (len(kbufs) + len(vbufs))
        + ([] if first else [VMEM] * 3 + [HBM]),
        out_specs=out_specs,
        scratch_shapes=([] if first else [pltpu.VMEM(s, jnp.float32) for s in running])
        + [pltpu.VMEM((MAXDOC, SPAN, HW), jnp.bfloat16)] * 2
        + [pltpu.VMEM((MAXDOC, 16, HW), jnp.bfloat16)] * 2
        + [pltpu.VMEM((SPAN, HW), jnp.bfloat16)]
        + [pltpu.SemaphoreType.DMA((MAXDOC,))] * 6,
        input_output_aliases={} if first else {fixed + 3: 1},
        compiler_params=pltpu.CompilerParams(vmem_limit_bytes=32 * 1024 * 1024),
        cost_estimate=pl.CostEstimate(
            flops=4 * lanes * HW * documents * SPAN,
            bytes_accessed=8 * documents * SPAN * HW,
            transcendentals=lanes * documents * SPAN,
        ),
    )(table, counts, pos, turns, new, qt, *kbufs, *vbufs, *state)


def on_device(
    kv_store,
    kv_scale,
    span_home,
    doc_ids,
    doc_count,
    recompute_rows,
    query_len,
    hidden,
    norm_gain,
    w_q,
    w_kv,
):
    tie = lax.optimization_barrier
    me = lax.axis_index("store")
    my_x, my_z = me // NZ, me % NZ

    scale_rows = jnp.transpose(kv_scale[:, :, 0, :], (1, 0, 2)).reshape(2, -1, 1)
    scale_rows = jnp.pad(scale_rows, ((0, 0), (0, 16 - 2 * STORED), (0, 0)))
    own = jnp.concatenate(
        [
            jnp.transpose(kv_store, (1, 0, 2, 3)).reshape(2, STORED * SPAN, HW),
            jnp.broadcast_to(scale_rows, (2, 16, HW)),
        ],
        axis=1,
    ).reshape(2 * BLOCK, HW)

    def keys_of(a):
        return a[:BLOCK]

    def values_of(a):
        return a[BLOCK:]

    def last_hop(a, b, dx, dz):
        left = pack([a], [(0, 0, CUT), (0, 2 * BLOCK - 16, 16)])
        right = pack([b], [(0, CUT, 2 * BLOCK + BLOCK - CUT)])
        return shift(left, dx, dz), shift(right, -dx, -dz)

    z1m, z1p = shift(own, 0, 1), shift(own, 0, -1)
    x1m, x1p = shift(own, 1, 0), shift(own, -1, 0)
    z1m, z1p, x1m, x1p = tie((z1m, z1p, x1m, x1p))
    z2m, z2p = shift(z1m, 0, 1), shift(z1p, 0, -1)
    x2k, x2v = shift(keys_of(x1m), 1, 0), shift(values_of(x1p), -1, 0)
    w0 = pack([x1m, x1p, x2v], [(0, BLOCK, BLOCK), (1, BLOCK, BLOCK), (2, 0, BLOCK)])
    w1m, w1p = shift(w0, 0, 1), shift(w0, 0, -1)
    z3m, z3p = shift(z2m, 0, 1), shift(z2p, 0, -1)
    d1 = pack([z1m, z1p, z2m, z2p], [(n, 0, BLOCK) for n in range(4)])
    d1m, d1p = shift(d1, 1, 0), shift(d1, -1, 0)
    w2m, w2p = shift(w1m, 0, 1), shift(w1p, 0, -1)
    z4k, z4v = shift(keys_of(z3m), 0, 1), shift(values_of(z3p), 0, -1)
    d1a, d1b = shift(d1m[: 2 * BLOCK], 1, 0), shift(d1p[2 * BLOCK :], -1, 0)
    d2 = pack([z3m, z3p, z4k], [(n, 0, BLOCK) for n in range(3)])
    d2m, d2p = shift(d2, 1, 0), shift(d2, -1, 0)

    doc_list = doc_ids[0]
    doc_total = doc_count[0]
    span_index = jnp.arange(span_home.shape[0], dtype=jnp.int32)
    position = jnp.sum(
        jnp.where(doc_list[:, None] == span_index[None, :], span_home[None, :], 0), axis=1
    )
    owner, slot = position // STORED, position % STORED
    dx = (owner // NZ - my_x) % NX
    dz = (owner % NZ - my_z) % NZ
    one_x = jnp.where(dx == 3, 0, dx)
    one_z = jnp.where(dz == 4, 6, jnp.where(dz > 4, 14 - 2 * dz, 2 * dz - 1))

    def split(block):
        second = (block == 2) | ((block == 1) & (slot == 2))
        row = block * BLOCK + slot * SPAN
        scale = jnp.where(block == 1, CUT, block * BLOCK + STORED * SPAN)
        scale_second = block * BLOCK + STORED * SPAN - CUT
        return (
            second.astype(jnp.int32),
            jnp.where(second, row - CUT, row),
            jnp.where(second, scale_second, scale),
        )

    live = jnp.arange(MAXDOC) < doc_total
    axis_buf = jnp.where(dx == 0, jnp.where(dz == 0, 0, 3 + one_z), jnp.where(dx == 2, 9, 1 + one_x))
    straight = (dx == 0) | (dz == 0)
    late = ((dx == 0) & (dz == 4)) | ((dx != 0) & (one_z >= 4))
    key_block = jnp.where(one_z >= 4, one_z - 4, one_z)
    piece, cut_row, cut_scale = split(key_block)
    kb = jnp.where(straight, axis_buf, 10 + one_x)
    row = slot * SPAN
    krow = jnp.where(straight, row, key_block * BLOCK + row)
    far = (~straight) & (dx == 2) & (key_block >= 2)
    kb = jnp.where(far, 13, kb)
    krow = jnp.where(far, krow - 2 * BLOCK, krow)
    ksc = krow - row + STORED * SPAN
    cut = late & (dx == 2)
    kb = jnp.where(late, jnp.where(dx == 0, 0, jnp.where(cut, 3 + piece, 1 + one_x)), kb)
    krow = jnp.where(late, jnp.where(cut, cut_row, jnp.where(dx == 0, row, key_block * BLOCK + row)), krow)
    ksc = jnp.where(late, jnp.where(cut, cut_scale, krow - row + STORED * SPAN), ksc)
    piece, cut_row, cut_scale = split(one_x)
    vb = jnp.where(straight, axis_buf, 10 + one_z)
    vrow = jnp.where(straight, jnp.where((dz == 0) & (dx == 2), row, BLOCK + row), one_x * BLOCK + row)
    vsc = vrow - row + STORED * SPAN
    cut = late & (dx != 0) & (dz == 4)
    vb = jnp.where(late, jnp.where(dx == 0, 0, jnp.where(cut, 3 + piece, one_z - 3)), vb)
    vrow = jnp.where(late, jnp.where(cut, cut_row, jnp.where(dx == 0, row, one_x * BLOCK + row)), vrow)
    vsc = jnp.where(late, jnp.where(cut, cut_scale, vrow - row + STORED * SPAN), vsc)
    facts = jnp.stack([jnp.arange(MAXDOC), slot, kb, krow, ksc, vb, vrow, vsc]).astype(jnp.int32)

    def chosen(flag):
        rank = jnp.sum(jnp.where(jnp.tri(MAXDOC, k=-1, dtype=bool) & flag[None, :], 1, 0), axis=1)
        seat = flag[:, None] & (rank[:, None] == jnp.arange(MAXDOC)[None, :])
        return jnp.sum(jnp.where(seat[None], facts[:, :, None], 0), axis=1)

    early_table, late_table = chosen(live & ~late), chosen(live & late)
    early_count = jnp.sum((live & ~late).astype(jnp.int32))
    counts = jnp.stack([doc_total, query_len[0], early_count, doc_total - early_count]).astype(
        jnp.int32
    )

    shift_cos, shift_sin = rope_angles(jnp.arange(MAXDOC, dtype=jnp.int32) * SPAN, HW)
    turns = jnp.stack(
        [
            jnp.concatenate([shift_cos, shift_cos], axis=1),
            jnp.concatenate([-shift_sin, shift_sin], axis=1),
        ],
        axis=1,
    )

    recompute_total = recompute_rows.shape[1] * recompute_rows.shape[2]
    flat_pos = recompute_rows[0].reshape(recompute_total).astype(jnp.int32)
    query_pos = doc_total * SPAN + jnp.arange(hidden.shape[1] - recompute_total, dtype=jnp.int32)
    row_cos, row_sin = rope_angles(jnp.concatenate([flat_pos, query_pos]), HW)
    layer_input = lax.all_gather(hidden, "tp", axis=2, tiled=True)[0]
    new, qt = project(
        layer_input,
        norm_gain[None],
        w_q,
        w_kv.reshape(w_kv.shape[0], 2 * HW),
        jnp.concatenate([row_cos, row_cos], axis=1),
        jnp.concatenate([-row_sin, row_sin], axis=1),
    )

    w2m, w2p, new, qt = tie((w2m, w2p, new, qt))
    w3m, w3p = shift(w2m, 0, 1), shift(w2p, 0, -1)
    straight_bufs = [own, x1m, x1p, z1m, z1p, z2m, z2p, z3m, z3p]
    common = (counts, flat_pos[None], turns, new, qt)
    context, *state = attend(
        True,
        straight_bufs + [x2k, d1m, d1p, d1a, d1b],
        straight_bufs + [x2v, w1m, w1p, w2m, w2p],
        early_table,
        *common,
        [],
    )
    w3m, w3p, d2m, d2p, state = tie((w3m, w3p, d2m, d2p, state))
    w4a, w4b = last_hop(w3m, w3p, 0, 1)
    d2a, d2b = last_hop(d2m, d2p, 1, 0)
    attention, context = attend(
        False,
        [z4k, d2m, d2p, d2a, d2b],
        [z4v, w3m, w3p, w4a, w4b],
        late_table,
        *common,
        [*state, context],
    )
    return (attention[None], context[None])


def solution(mesh):
    placed = (
        P("store", None, None, "tp"),
        P("store", None, "tp", None),
        P(),
        P("store", None),
        P("store"),
        P("store", None, None),
        P("store"),
        P("store", None, "tp"),
        P(),
        P(None, "tp"),
        P(None, None, "tp"),
    )
    return jax.shard_map(
        on_device,
        mesh=mesh,
        in_specs=placed,
        out_specs=(P("store", None, "tp"), P("store", None, None, "tp")),
        check_vma=False,
    )
```

```python
import functools
import jax
import jax.numpy as jnp
from jax import lax
from jax.experimental import pallas as pl
from jax.experimental.pallas import tpu as pltpu
from jax.sharding import PartitionSpec as P

SPAN = 256
SB = 128
MAXDOC = 20
NX, NZ = 4, 8
HW = 128
LOG2E = 1.4426950408889634
STORED = 3
BLOCK = STORED * SPAN + 16
CUT = BLOCK + 2 * SPAN
ROOM = 20 * 1024 * 1024


rope_base = 500000.0
norm_eps = 1e-05


def rope_angles(positions, head_width):
    halfway = head_width // 2
    exponent = jnp.arange(halfway, dtype=jnp.float32) * (2.0 / head_width)
    inverse_freq = jnp.power(jnp.float32(rope_base), -exponent)
    angles = positions.astype(jnp.float32)[:, None] * inverse_freq[None, :]
    return (jnp.cos(angles), jnp.sin(angles))


def rotate_half(values, cosine, sine_part):
    halfway = values.shape[-1] // 2
    low_half = values[..., :halfway]
    high_half = values[..., halfway:]
    return jnp.concatenate(
        [low_half * cosine - high_half * sine_part, high_half * cosine + low_half * sine_part],
        axis=-1,
    )


def shift(a, dx, dz):
    pairs = [
        (x * NZ + z, ((x + dx) % NX) * NZ + (z + dz) % NZ) for x in range(NX) for z in range(NZ)
    ]
    return lax.ppermute(a, "store", pairs)


HBM = pl.BlockSpec(memory_space=pl.ANY)
VMEM = pl.BlockSpec(memory_space=pltpu.VMEM)
SMEM = pl.BlockSpec(memory_space=pltpu.SMEM)


def pack_kernel(plan, *refs):
    sources, out = refs[:-1], refs[-1]
    at = 0
    for source, start, rows in plan:
        out[at : at + rows] = sources[source][start : start + rows]
        at += rows


def pack(sources, plan):
    rows = sum(p[2] for p in plan)
    return pl.pallas_call(
        functools.partial(pack_kernel, plan),
        out_shape=jax.ShapeDtypeStruct((rows, HW), jnp.bfloat16),
        in_specs=[VMEM] * len(sources),
        out_specs=VMEM,
        compiler_params=pltpu.CompilerParams(vmem_limit_bytes=2 * 1024 * 1024),
        cost_estimate=pl.CostEstimate(
            flops=0, bytes_accessed=4 * rows * HW, transcendentals=0
        ),
    )(*sources)


def project_kernel(hid_ref, gain_ref, wq_ref, wkv_ref, cos_ref, sin_ref, new_ref, qt_ref, nb_ref):
    features = hid_ref.shape[1]
    piece = 512
    total = jnp.zeros((SPAN, 1), jnp.float32)
    for c in range(0, features, piece):
        x = hid_ref[:, c : c + piece].astype(jnp.float32)
        total = total + jnp.sum(x * x, axis=1, keepdims=True)
    inverse = lax.rsqrt(total * (1.0 / features) + norm_eps)
    for c in range(0, features, piece):
        x = hid_ref[:, c : c + piece].astype(jnp.float32)
        gain = gain_ref[:, c : c + piece].astype(jnp.float32)
        nb_ref[:, c : c + piece] = (x * inverse * gain).astype(jnp.bfloat16)
    kv = jnp.dot(nb_ref[...], wkv_ref[...], preferred_element_type=jnp.float32)
    cosine, sine = cos_ref[...], sin_ref[...]
    k = kv[:, :HW]
    new_ref[:, :HW] = (k * cosine + pltpu.roll(k, HW // 2, 1) * sine).astype(jnp.bfloat16)
    new_ref[:, HW : 2 * HW] = kv[:, HW:].astype(jnp.bfloat16)
    new_ref[:, 2 * HW :] = jnp.ones((SPAN, HW), jnp.bfloat16)

    @pl.when(pl.program_id(0) == pl.num_programs(0) - 1)
    def _():
        q = jnp.dot(nb_ref[...], wq_ref[...], preferred_element_type=jnp.float32)
        for h in range(q.shape[1] // HW):
            one = q[:, h * HW : (h + 1) * HW]
            one = one * cosine + pltpu.roll(one, HW // 2, 1) * sine
            qt_ref[:, h * SPAN : (h + 1) * SPAN] = one.T.astype(jnp.bfloat16)


def project(hid, gain, wq, wkv, cosine, sine):
    rows, features = hid.shape
    lanes = wq.shape[1] // HW * SPAN
    return pl.pallas_call(
        project_kernel,
        grid=(rows // SPAN,),
        out_shape=(
            jax.ShapeDtypeStruct((rows, 3 * HW), jnp.bfloat16),
            jax.ShapeDtypeStruct((HW, lanes), jnp.bfloat16),
        ),
        in_specs=[
            pl.BlockSpec((SPAN, features), lambda i: (i, 0)),
            pl.BlockSpec((1, features), lambda i: (0, 0)),
            pl.BlockSpec(wq.shape, lambda i: (0, 0), pipeline_mode=pl.Buffered(1)),
            pl.BlockSpec(wkv.shape, lambda i: (0, 0), pipeline_mode=pl.Buffered(1)),
            pl.BlockSpec((SPAN, HW), lambda i: (i, 0)),
            pl.BlockSpec((SPAN, HW), lambda i: (i, 0)),
        ],
        out_specs=(
            pl.BlockSpec((SPAN, 3 * HW), lambda i: (i, 0)),
            pl.BlockSpec((HW, lanes), lambda i: (0, 0)),
        ),
        scratch_shapes=[pltpu.VMEM((SPAN, features), jnp.bfloat16)],
        compiler_params=pltpu.CompilerParams(vmem_limit_bytes=ROOM),
        cost_estimate=pl.CostEstimate(
            flops=2 * features * HW * (2 * rows + 4 * SPAN),
            bytes_accessed=2 * features * (rows + 6 * HW),
            transcendentals=0,
        ),
    )(hid, gain, wq, wkv, cosine, sine)


DOC, SLOT, KB, KROW, KSC, VB, VROW, VSC = range(8)


def attend_kernel(first, nk, nv, table, count_ref, pos_ref, shift_ref, new_ref, qt_ref, *refs):
    kbufs, vbufs, refs = refs[:nk], refs[nk : nk + nv], refs[nk + nv :]
    if first:
        ctx_ref, m_ref, l_ref, acc_ref = refs[:4]
        refs = refs[4:]
    else:
        m_in, l_in, acc_in, _, out_ref, ctx_ref, m_ref, l_ref, acc_ref = refs[:9]
        refs = refs[9:]
    kdoc, vdoc, kscale, vscale, zero, ksem, vsem, kssem, vssem, kout, vout = refs
    count = count_ref[2] if first else count_ref[3]
    lanes = qt_ref.shape[1]
    nrec = pos_ref.shape[1]
    factor = HW**-0.5 * LOG2E
    heads = [slice(h, h + SPAN) for h in range(0, lanes, SPAN)]

    def pick(n, low, high, act):
        if high - low == 1:
            act(low)
            return
        mid = (low + high) // 2

        @pl.when(n < mid)
        def _():
            pick(n, low, mid, act)

        @pl.when(n >= mid)
        def _():
            pick(n, mid, high, act)

    def fetch(r, _):
        def keys(b):
            row = pl.multiple_of(table[KROW, r], 16)
            pltpu.make_async_copy(kbufs[b].at[pl.ds(row, SPAN)], kdoc.at[r], ksem.at[r]).start()
            row = pl.multiple_of(table[KSC, r], 16)
            pltpu.make_async_copy(kbufs[b].at[pl.ds(row, 16)], kscale.at[r], kssem.at[r]).start()

        def values(b):
            row = pl.multiple_of(table[VROW, r], 16)
            pltpu.make_async_copy(vbufs[b].at[pl.ds(row, SPAN)], vdoc.at[r], vsem.at[r]).start()
            row = pl.multiple_of(table[VSC, r], 16)
            pltpu.make_async_copy(vbufs[b].at[pl.ds(row, 16)], vscale.at[r], vssem.at[r]).start()

        pick(table[KB, r], 0, nk, keys)
        pick(table[VB, r], 0, nv, values)
        return 0

    lax.fori_loop(0, count, fetch, 0)

    def place(j):
        return pl.ds(pl.multiple_of(j * SPAN, SPAN), SPAN)

    if first:
        docs = count_ref[0]
        zero[...] = jnp.zeros(zero.shape, zero.dtype)

        def blank(j, _):
            pltpu.make_async_copy(zero, ctx_ref.at[0, place(j)], kout.at[j]).start()
            pltpu.make_async_copy(zero, ctx_ref.at[1, place(j)], vout.at[j]).start()
            return 0

        lax.fori_loop(docs, MAXDOC, blank, 0)

        own_keys = new_ref[nrec:, :HW]
        own_values = new_ref[nrec:, HW : 2 * HW]
        for h in heads:
            scores = jnp.dot(own_keys, qt_ref[:, h], preferred_element_type=jnp.float32)
            key_index = lax.broadcasted_iota(jnp.int32, scores.shape, 0)
            query_index = lax.broadcasted_iota(jnp.int32, scores.shape, 1)
            scores = jnp.where(key_index <= query_index, scores, -jnp.inf)
            top = jnp.max(scores, axis=0, keepdims=True)
            terms = jnp.exp2((scores - top) * factor)
            m_ref[:, h] = top
            l_ref[:, h] = jnp.sum(terms, axis=0, keepdims=True)
            acc_ref[:, h] = lax.dot_general(
                own_values,
                terms.astype(jnp.bfloat16),
                (((0,), (0,)), ((), ())),
                preferred_element_type=jnp.float32,
            )
    else:
        m_ref[...] = m_in[...]
        l_ref[...] = l_in[...]
        acc_ref[...] = acc_in[...]

    upper = lax.broadcasted_iota(jnp.int32, (SPAN, HW), 0) >= SB
    row_index = lax.broadcasted_iota(jnp.int32, (SPAN, nrec), 0)
    scale_index = lax.broadcasted_iota(jnp.int32, (16, HW), 0)

    def dequant(codes, scales, slot):
        s = scales.astype(jnp.float32)
        low = jnp.sum(jnp.where(scale_index == 2 * slot, s, 0.0), axis=0, keepdims=True)
        high = jnp.sum(jnp.where(scale_index == 2 * slot + 1, s, 0.0), axis=0, keepdims=True)
        return codes.astype(jnp.float32) * jnp.where(upper, high, low)

    def step(r, _):
        j, slot = table[DOC, r], table[SLOT, r]
        hit = jnp.where(row_index == pos_ref[...] - j * SPAN, 1.0, 0.0).astype(jnp.bfloat16)
        fresh = jnp.dot(hit, new_ref[:nrec], preferred_element_type=jnp.float32)
        replaced = fresh[:, 2 * HW :] > 0.5
        pltpu.make_async_copy(kbufs[0].at[pl.ds(0, SPAN)], kdoc.at[r], ksem.at[r]).wait()
        pltpu.make_async_copy(kbufs[0].at[pl.ds(0, 16)], kscale.at[r], kssem.at[r]).wait()
        pltpu.make_async_copy(vbufs[0].at[pl.ds(0, SPAN)], vdoc.at[r], vsem.at[r]).wait()
        pltpu.make_async_copy(vbufs[0].at[pl.ds(0, 16)], vscale.at[r], vssem.at[r]).wait()
        k = dequant(kdoc[r], kscale[r], slot)
        turn = shift_ref[j]
        k = k * turn[0:1] + pltpu.roll(k, HW // 2, 1) * turn[1:2]
        k = jnp.where(replaced, fresh[:, :HW], k).astype(jnp.bfloat16)
        v = dequant(vdoc[r], vscale[r], slot)
        v = jnp.where(replaced, fresh[:, HW : 2 * HW], v).astype(jnp.bfloat16)
        kdoc[r] = k
        vdoc[r] = v
        pltpu.make_async_copy(kdoc.at[r], ctx_ref.at[0, place(j)], kout.at[r]).start()
        pltpu.make_async_copy(vdoc.at[r], ctx_ref.at[1, place(j)], vout.at[r]).start()
        for h in heads:
            scores = jnp.dot(k, qt_ref[:, h], preferred_element_type=jnp.float32)
            before = m_ref[:, h]
            top = jnp.maximum(before, jnp.max(scores, axis=0, keepdims=True))
            terms = jnp.exp2((scores - top) * factor)
            fade = jnp.exp2((before - top) * factor)
            m_ref[:, h] = top
            l_ref[:, h] = l_ref[:, h] * fade + jnp.sum(terms, axis=0, keepdims=True)
            acc_ref[:, h] = acc_ref[:, h] * fade + lax.dot_general(
                v,
                terms.astype(jnp.bfloat16),
                (((0,), (0,)), ((), ())),
                preferred_element_type=jnp.float32,
            )
        return 0

    lax.fori_loop(0, count, step, 0)

    if not first:
        live = lax.broadcasted_iota(jnp.int32, (1, SPAN), 1) < count_ref[1]
        for n, h in enumerate(heads):
            mixed = jnp.where(live, acc_ref[:, h] / l_ref[:, h], 0.0)
            out_ref[:, n * HW : (n + 1) * HW] = mixed.T.astype(jnp.bfloat16)

    def finish(r, _):
        pltpu.make_async_copy(kdoc.at[0], ctx_ref.at[0, pl.ds(0, SPAN)], kout.at[r]).wait()
        pltpu.make_async_copy(vdoc.at[0], ctx_ref.at[1, pl.ds(0, SPAN)], vout.at[r]).wait()
        return 0

    lax.fori_loop(0, count, finish, 0)
    if first:
        lax.fori_loop(count_ref[0], MAXDOC, finish, 0)


def attend(first, kbufs, vbufs, table, counts, pos, turns, new, qt, state):
    lanes = qt.shape[1]
    context = jax.ShapeDtypeStruct((2, MAXDOC * SPAN, HW), jnp.bfloat16)
    running = [(1, lanes), (1, lanes), (HW, lanes)]
    if first:
        out_shape = (context, *[jax.ShapeDtypeStruct(s, jnp.float32) for s in running])
        out_specs = (HBM, VMEM, VMEM, VMEM)
    else:
        out_shape = (jax.ShapeDtypeStruct((SPAN, lanes // SPAN * HW), jnp.bfloat16), context)
        out_specs = (VMEM, HBM)
    fixed = 6 + len(kbufs) + len(vbufs)
    documents = MAXDOC // 2
    return pl.pallas_call(
        functools.partial(attend_kernel, first, len(kbufs), len(vbufs)),
        out_shape=out_shape,
        in_specs=[SMEM] * 2
        + [VMEM] * 4
        + [HBM] * (len(kbufs) + len(vbufs))
        + ([] if first else [VMEM] * 3 + [HBM]),
        out_specs=out_specs,
        scratch_shapes=([] if first else [pltpu.VMEM(s, jnp.float32) for s in running])
        + [pltpu.VMEM((MAXDOC, SPAN, HW), jnp.bfloat16)] * 2
        + [pltpu.VMEM((MAXDOC, 16, HW), jnp.bfloat16)] * 2
        + [pltpu.VMEM((SPAN, HW), jnp.bfloat16)]
        + [pltpu.SemaphoreType.DMA((MAXDOC,))] * 6,
        input_output_aliases={} if first else {fixed + 3: 1},
        compiler_params=pltpu.CompilerParams(vmem_limit_bytes=ROOM),
        cost_estimate=pl.CostEstimate(
            flops=4 * lanes * HW * documents * SPAN,
            bytes_accessed=8 * documents * SPAN * HW,
            transcendentals=lanes * documents * SPAN,
        ),
    )(table, counts, pos, turns, new, qt, *kbufs, *vbufs, *state)


def on_device(
    kv_store,
    kv_scale,
    span_home,
    doc_ids,
    doc_count,
    recompute_rows,
    query_len,
    hidden,
    norm_gain,
    w_q,
    w_kv,
):
    tie = lax.optimization_barrier
    me = lax.axis_index("store")
    my_x, my_z = me // NZ, me % NZ

    scale_rows = jnp.transpose(kv_scale[:, :, 0, :], (1, 0, 2)).reshape(2, -1, 1)
    scale_rows = jnp.pad(scale_rows, ((0, 0), (0, 16 - 2 * STORED), (0, 0)))
    own = jnp.concatenate(
        [
            jnp.transpose(kv_store, (1, 0, 2, 3)).reshape(2, STORED * SPAN, HW),
            jnp.broadcast_to(scale_rows, (2, 16, HW)),
        ],
        axis=1,
    ).reshape(2 * BLOCK, HW)

    def keys_of(a):
        return pack([a], [(0, 0, BLOCK)])

    def values_of(a):
        return pack([a], [(0, BLOCK, BLOCK)])

    def last_hop(a, b, dx, dz):
        left = pack([a], [(0, 0, CUT), (0, 2 * BLOCK - 16, 16)])
        right = pack([b], [(0, CUT, 2 * BLOCK + BLOCK - CUT)])
        return shift(left, dx, dz), shift(right, -dx, -dz)

    z1m, z1p = shift(own, 0, 1), shift(own, 0, -1)
    x1m, x1p = shift(own, 1, 0), shift(own, -1, 0)
    z1m, z1p, x1m, x1p = tie((z1m, z1p, x1m, x1p))
    z2m, z2p = shift(z1m, 0, 1), shift(z1p, 0, -1)
    x2k, x2v = shift(keys_of(x1m), 1, 0), shift(values_of(x1p), -1, 0)
    w0 = pack([x1m, x1p, x2v], [(0, BLOCK, BLOCK), (1, BLOCK, BLOCK), (2, 0, BLOCK)])
    w1m, w1p = shift(w0, 0, 1), shift(w0, 0, -1)
    z3m, z3p = shift(z2m, 0, 1), shift(z2p, 0, -1)
    d1 = pack([z1m, z1p, z2m, z2p], [(n, 0, BLOCK) for n in range(4)])
    d1m, d1p = shift(d1, 1, 0), shift(d1, -1, 0)
    w2m, w2p = shift(w1m, 0, 1), shift(w1p, 0, -1)
    z4k, z4v = shift(keys_of(z3m), 0, 1), shift(values_of(z3p), 0, -1)
    d1a = shift(pack([d1m], [(0, 0, 2 * BLOCK)]), 1, 0)
    d1b = shift(pack([d1p], [(0, 2 * BLOCK, 2 * BLOCK)]), -1, 0)
    d2 = pack([z3m, z3p, z4k], [(n, 0, BLOCK) for n in range(3)])
    d2m, d2p = shift(d2, 1, 0), shift(d2, -1, 0)

    doc_list = doc_ids[0]
    doc_total = doc_count[0]
    span_index = jnp.arange(span_home.shape[0], dtype=jnp.int32)
    position = jnp.sum(
        jnp.where(doc_list[:, None] == span_index[None, :], span_home[None, :], 0), axis=1
    )
    owner, slot = position // STORED, position % STORED
    dx = (owner // NZ - my_x) % NX
    dz = (owner % NZ - my_z) % NZ
    one_x = jnp.where(dx == 3, 0, dx)
    one_z = jnp.where(dz == 4, 6, jnp.where(dz > 4, 14 - 2 * dz, 2 * dz - 1))

    def split(block):
        second = (block == 2) | ((block == 1) & (slot == 2))
        row = block * BLOCK + slot * SPAN
        scale = jnp.where(block == 1, CUT, block * BLOCK + STORED * SPAN)
        scale_second = block * BLOCK + STORED * SPAN - CUT
        return (
            second.astype(jnp.int32),
            jnp.where(second, row - CUT, row),
            jnp.where(second, scale_second, scale),
        )

    live = jnp.arange(MAXDOC) < doc_total
    axis_buf = jnp.where(dx == 0, jnp.where(dz == 0, 0, 3 + one_z), jnp.where(dx == 2, 9, 1 + one_x))
    straight = (dx == 0) | (dz == 0)
    late = ((dx == 0) & (dz == 4)) | ((dx != 0) & (one_z >= 4))
    key_block = jnp.where(one_z >= 4, one_z - 4, one_z)
    piece, cut_row, cut_scale = split(key_block)
    kb = jnp.where(straight, axis_buf, 10 + one_x)
    row = slot * SPAN
    krow = jnp.where(straight, row, key_block * BLOCK + row)
    far = (~straight) & (dx == 2) & (key_block >= 2)
    kb = jnp.where(far, 13, kb)
    krow = jnp.where(far, krow - 2 * BLOCK, krow)
    ksc = krow - row + STORED * SPAN
    cut = late & (dx == 2)
    kb = jnp.where(late, jnp.where(dx == 0, 0, jnp.where(cut, 3 + piece, 1 + one_x)), kb)
    krow = jnp.where(late, jnp.where(cut, cut_row, jnp.where(dx == 0, row, key_block * BLOCK + row)), krow)
    ksc = jnp.where(late, jnp.where(cut, cut_scale, krow - row + STORED * SPAN), ksc)
    piece, cut_row, cut_scale = split(one_x)
    vb = jnp.where(straight, axis_buf, 10 + one_z)
    vrow = jnp.where(straight, jnp.where((dz == 0) & (dx == 2), row, BLOCK + row), one_x * BLOCK + row)
    vsc = vrow - row + STORED * SPAN
    cut = late & (dx != 0) & (dz == 4)
    vb = jnp.where(late, jnp.where(dx == 0, 0, jnp.where(cut, 3 + piece, one_z - 3)), vb)
    vrow = jnp.where(late, jnp.where(cut, cut_row, jnp.where(dx == 0, row, one_x * BLOCK + row)), vrow)
    vsc = jnp.where(late, jnp.where(cut, cut_scale, vrow - row + STORED * SPAN), vsc)
    facts = jnp.stack([jnp.arange(MAXDOC), slot, kb, krow, ksc, vb, vrow, vsc]).astype(jnp.int32)

    def chosen(flag):
        rank = jnp.sum(jnp.where(jnp.tri(MAXDOC, k=-1, dtype=bool) & flag[None, :], 1, 0), axis=1)
        seat = flag[:, None] & (rank[:, None] == jnp.arange(MAXDOC)[None, :])
        return jnp.sum(jnp.where(seat[None], facts[:, :, None], 0), axis=1)

    early_table, late_table = chosen(live & ~late), chosen(live & late)
    early_count = jnp.sum((live & ~late).astype(jnp.int32))
    counts = jnp.stack([doc_total, query_len[0], early_count, doc_total - early_count]).astype(
        jnp.int32
    )

    shift_cos, shift_sin = rope_angles(jnp.arange(MAXDOC, dtype=jnp.int32) * SPAN, HW)
    turns = jnp.stack(
        [
            jnp.concatenate([shift_cos, shift_cos], axis=1),
            jnp.concatenate([-shift_sin, shift_sin], axis=1),
        ],
        axis=1,
    )

    recompute_total = recompute_rows.shape[1] * recompute_rows.shape[2]
    flat_pos = recompute_rows[0].reshape(recompute_total).astype(jnp.int32)
    query_pos = doc_total * SPAN + jnp.arange(hidden.shape[1] - recompute_total, dtype=jnp.int32)
    row_cos, row_sin = rope_angles(jnp.concatenate([flat_pos, query_pos]), HW)
    layer_input = lax.all_gather(hidden, "tp", axis=2, tiled=True)[0]
    new, qt = project(
        layer_input,
        norm_gain[None],
        w_q,
        w_kv.reshape(w_kv.shape[0], 2 * HW),
        jnp.concatenate([row_cos, row_cos], axis=1),
        jnp.concatenate([-row_sin, row_sin], axis=1),
    )

    w2m, w2p, new, qt = tie((w2m, w2p, new, qt))
    w3m, w3p = shift(w2m, 0, 1), shift(w2p, 0, -1)
    straight_bufs = [own, x1m, x1p, z1m, z1p, z2m, z2p, z3m, z3p]
    common = (counts, flat_pos[None], turns, new, qt)
    context, *state = attend(
        True,
        straight_bufs + [x2k, d1m, d1p, d1a, d1b],
        straight_bufs + [x2v, w1m, w1p, w2m, w2p],
        early_table,
        *common,
        [],
    )
    w3m, w3p, d2m, d2p, state = tie((w3m, w3p, d2m, d2p, state))
    w4a, w4b = last_hop(w3m, w3p, 0, 1)
    d2a, d2b = last_hop(d2m, d2p, 1, 0)
    attention, context = attend(
        False,
        [z4k, d2m, d2p, d2a, d2b],
        [z4v, w3m, w3p, w4a, w4b],
        late_table,
        *common,
        [*state, context],
    )
    return (attention[None], context[None])


def solution(mesh):
    placed = (
        P("store", None, None, "tp"),
        P("store", None, "tp", None),
        P(),
        P("store", None),
        P("store"),
        P("store", None, None),
        P("store"),
        P("store", None, "tp"),
        P(),
        P(None, "tp"),
        P(None, None, "tp"),
    )
    return jax.shard_map(
        on_device,
        mesh=mesh,
        in_specs=placed,
        out_specs=(P("store", None, "tp"), P("store", None, None, "tp")),
        check_vma=False,
    )
```

```python
import functools
import jax
import jax.numpy as jnp
from jax import lax
from jax.experimental import pallas as pl
from jax.experimental.pallas import tpu as pltpu
from jax.sharding import PartitionSpec as P

SPAN = 256
SB = 128
MAXDOC = 20
NX, NZ = 4, 8
HW = 128
LOG2E = 1.4426950408889634
STORED = 3
BLOCK = STORED * SPAN + 16
CUT = BLOCK + 2 * SPAN
ROOM = 20 * 1024 * 1024


rope_base = 500000.0
norm_eps = 1e-05


def rope_angles(positions, head_width):
    halfway = head_width // 2
    exponent = jnp.arange(halfway, dtype=jnp.float32) * (2.0 / head_width)
    inverse_freq = jnp.power(jnp.float32(rope_base), -exponent)
    angles = positions.astype(jnp.float32)[:, None] * inverse_freq[None, :]
    return (jnp.cos(angles), jnp.sin(angles))


def rotate_half(values, cosine, sine_part):
    halfway = values.shape[-1] // 2
    low_half = values[..., :halfway]
    high_half = values[..., halfway:]
    return jnp.concatenate(
        [low_half * cosine - high_half * sine_part, high_half * cosine + low_half * sine_part],
        axis=-1,
    )


def shift(a, dx, dz):
    pairs = [
        (x * NZ + z, ((x + dx) % NX) * NZ + (z + dz) % NZ) for x in range(NX) for z in range(NZ)
    ]
    return lax.ppermute(a, "store", pairs)


HBM = pl.BlockSpec(memory_space=pl.ANY)
KEPT = pl.BlockSpec(memory_space=pltpu.HBM)
VMEM = pl.BlockSpec(memory_space=pltpu.VMEM)
SMEM = pl.BlockSpec(memory_space=pltpu.SMEM)


def pack_kernel(plan, *refs):
    sources, out = refs[:-1], refs[-1]
    at = 0
    for source, start, rows in plan:
        out[at : at + rows] = sources[source][start : start + rows]
        at += rows


def pack(sources, plan):
    rows = sum(p[2] for p in plan)
    return pl.pallas_call(
        functools.partial(pack_kernel, plan),
        out_shape=jax.ShapeDtypeStruct((rows, HW), jnp.bfloat16),
        in_specs=[VMEM] * len(sources),
        out_specs=VMEM,
        compiler_params=pltpu.CompilerParams(vmem_limit_bytes=2 * 1024 * 1024),
        cost_estimate=pl.CostEstimate(
            flops=0, bytes_accessed=4 * rows * HW, transcendentals=0
        ),
    )(*sources)


def project_kernel(hid_ref, gain_ref, wq_ref, wkv_ref, cos_ref, sin_ref, new_ref, qt_ref, nb_ref):
    features = hid_ref.shape[1]
    piece = 512
    total = jnp.zeros((SPAN, 1), jnp.float32)
    for c in range(0, features, piece):
        x = hid_ref[:, c : c + piece].astype(jnp.float32)
        total = total + jnp.sum(x * x, axis=1, keepdims=True)
    inverse = lax.rsqrt(total * (1.0 / features) + norm_eps)
    for c in range(0, features, piece):
        x = hid_ref[:, c : c + piece].astype(jnp.float32)
        gain = gain_ref[:, c : c + piece].astype(jnp.float32)
        nb_ref[:, c : c + piece] = (x * inverse * gain).astype(jnp.bfloat16)
    kv = jnp.dot(nb_ref[...], wkv_ref[...], preferred_element_type=jnp.float32)
    cosine, sine = cos_ref[...], sin_ref[...]
    k = kv[:, :HW]
    new_ref[:, :HW] = (k * cosine + pltpu.roll(k, HW // 2, 1) * sine).astype(jnp.bfloat16)
    new_ref[:, HW : 2 * HW] = kv[:, HW:].astype(jnp.bfloat16)
    new_ref[:, 2 * HW :] = jnp.ones((SPAN, HW), jnp.bfloat16)

    @pl.when(pl.program_id(0) == pl.num_programs(0) - 1)
    def _():
        q = jnp.dot(nb_ref[...], wq_ref[...], preferred_element_type=jnp.float32)
        for h in range(q.shape[1] // HW):
            one = q[:, h * HW : (h + 1) * HW]
            one = one * cosine + pltpu.roll(one, HW // 2, 1) * sine
            qt_ref[:, h * SPAN : (h + 1) * SPAN] = one.T.astype(jnp.bfloat16)


def project(hid, gain, wq, wkv, cosine, sine):
    rows, features = hid.shape
    lanes = wq.shape[1] // HW * SPAN
    return pl.pallas_call(
        project_kernel,
        grid=(rows // SPAN,),
        out_shape=(
            jax.ShapeDtypeStruct((rows, 3 * HW), jnp.bfloat16),
            jax.ShapeDtypeStruct((HW, lanes), jnp.bfloat16),
        ),
        in_specs=[
            pl.BlockSpec((SPAN, features), lambda i: (i, 0)),
            pl.BlockSpec((1, features), lambda i: (0, 0)),
            pl.BlockSpec(wq.shape, lambda i: (0, 0), pipeline_mode=pl.Buffered(1)),
            pl.BlockSpec(wkv.shape, lambda i: (0, 0), pipeline_mode=pl.Buffered(1)),
            pl.BlockSpec((SPAN, HW), lambda i: (i, 0)),
            pl.BlockSpec((SPAN, HW), lambda i: (i, 0)),
        ],
        out_specs=(
            pl.BlockSpec((SPAN, 3 * HW), lambda i: (i, 0)),
            pl.BlockSpec((HW, lanes), lambda i: (0, 0)),
        ),
        scratch_shapes=[pltpu.VMEM((SPAN, features), jnp.bfloat16)],
        compiler_params=pltpu.CompilerParams(vmem_limit_bytes=ROOM),
        cost_estimate=pl.CostEstimate(
            flops=2 * features * HW * (2 * rows + 4 * SPAN),
            bytes_accessed=2 * features * (rows + 6 * HW),
            transcendentals=0,
        ),
    )(hid, gain, wq, wkv, cosine, sine)


DOC, SLOT, KB, KROW, KSC, VB, VROW, VSC = range(8)


def attend_kernel(first, nk, nv, table, count_ref, pos_ref, shift_ref, new_ref, qt_ref, *refs):
    kbufs, vbufs, refs = refs[:nk], refs[nk : nk + nv], refs[nk + nv :]
    if first:
        ctx_ref, m_ref, l_ref, acc_ref = refs[:4]
        refs = refs[4:]
    else:
        m_in, l_in, acc_in, _, out_ref, ctx_ref, m_ref, l_ref, acc_ref = refs[:9]
        refs = refs[9:]
    kdoc, vdoc, kscale, vscale, zero, ksem, vsem, kssem, vssem, kout, vout = refs
    count = count_ref[2] if first else count_ref[3]
    lanes = qt_ref.shape[1]
    nrec = pos_ref.shape[1]
    factor = HW**-0.5 * LOG2E
    heads = [slice(0, lanes)]

    def pick(n, low, high, act):
        if high - low == 1:
            act(low)
            return
        mid = (low + high) // 2

        @pl.when(n < mid)
        def _():
            pick(n, low, mid, act)

        @pl.when(n >= mid)
        def _():
            pick(n, mid, high, act)

    def fetch(r, _):
        def keys(b):
            row = pl.multiple_of(table[KROW, r], 16)
            pltpu.make_async_copy(kbufs[b].at[pl.ds(row, SPAN)], kdoc.at[r], ksem.at[r]).start()
            row = pl.multiple_of(table[KSC, r], 16)
            pltpu.make_async_copy(kbufs[b].at[pl.ds(row, 16)], kscale.at[r], kssem.at[r]).start()

        def values(b):
            row = pl.multiple_of(table[VROW, r], 16)
            pltpu.make_async_copy(vbufs[b].at[pl.ds(row, SPAN)], vdoc.at[r], vsem.at[r]).start()
            row = pl.multiple_of(table[VSC, r], 16)
            pltpu.make_async_copy(vbufs[b].at[pl.ds(row, 16)], vscale.at[r], vssem.at[r]).start()

        pick(table[KB, r], 0, nk, keys)
        pick(table[VB, r], 0, nv, values)
        return 0

    lax.fori_loop(0, count, fetch, 0)

    def place(j):
        return pl.ds(pl.multiple_of(j * SPAN, SPAN), SPAN)

    if first:
        docs = count_ref[0]
        zero[...] = jnp.zeros(zero.shape, zero.dtype)

        def blank(j, _):
            pltpu.make_async_copy(zero, ctx_ref.at[0, place(j)], kout.at[j]).start()
            pltpu.make_async_copy(zero, ctx_ref.at[1, place(j)], vout.at[j]).start()
            return 0

        lax.fori_loop(docs, MAXDOC, blank, 0)

        own_keys = new_ref[nrec:, :HW]
        own_values = new_ref[nrec:, HW : 2 * HW]
        for h in heads:
            scores = jnp.dot(own_keys, qt_ref[:, h], preferred_element_type=jnp.float32)
            key_index = lax.broadcasted_iota(jnp.int32, scores.shape, 0)
            query_index = lax.broadcasted_iota(jnp.int32, scores.shape, 1) & (SPAN - 1)
            scores = jnp.where(key_index <= query_index, scores, -jnp.inf)
            top = jnp.max(scores, axis=0, keepdims=True)
            terms = jnp.exp2((scores - top) * factor)
            m_ref[:, h] = top
            l_ref[:, h] = jnp.sum(terms, axis=0, keepdims=True)
            acc_ref[:, h] = lax.dot_general(
                own_values,
                terms.astype(jnp.bfloat16),
                (((0,), (0,)), ((), ())),
                preferred_element_type=jnp.float32,
            )
    else:
        m_ref[...] = m_in[...]
        l_ref[...] = l_in[...]
        acc_ref[...] = acc_in[...]

    upper = lax.broadcasted_iota(jnp.int32, (SPAN, HW), 0) >= SB
    row_index = lax.broadcasted_iota(jnp.int32, (SPAN, nrec), 0)
    scale_index = lax.broadcasted_iota(jnp.int32, (16, HW), 0)

    def dequant(codes, scales, slot):
        s = scales.astype(jnp.float32)
        low = jnp.sum(jnp.where(scale_index == 2 * slot, s, 0.0), axis=0, keepdims=True)
        high = jnp.sum(jnp.where(scale_index == 2 * slot + 1, s, 0.0), axis=0, keepdims=True)
        return codes.astype(jnp.float32) * jnp.where(upper, high, low)

    def step(r, _):
        j, slot = table[DOC, r], table[SLOT, r]
        hit = jnp.where(row_index == pos_ref[...] - j * SPAN, 1.0, 0.0).astype(jnp.bfloat16)
        fresh = jnp.dot(hit, new_ref[:nrec], preferred_element_type=jnp.float32)
        replaced = fresh[:, 2 * HW :] > 0.5
        pltpu.make_async_copy(kbufs[0].at[pl.ds(0, SPAN)], kdoc.at[r], ksem.at[r]).wait()
        pltpu.make_async_copy(kbufs[0].at[pl.ds(0, 16)], kscale.at[r], kssem.at[r]).wait()
        pltpu.make_async_copy(vbufs[0].at[pl.ds(0, SPAN)], vdoc.at[r], vsem.at[r]).wait()
        pltpu.make_async_copy(vbufs[0].at[pl.ds(0, 16)], vscale.at[r], vssem.at[r]).wait()
        k = dequant(kdoc[r], kscale[r], slot)
        turn = shift_ref[j]
        k = k * turn[0:1] + pltpu.roll(k, HW // 2, 1) * turn[1:2]
        k = jnp.where(replaced, fresh[:, :HW], k).astype(jnp.bfloat16)
        v = dequant(vdoc[r], vscale[r], slot)
        v = jnp.where(replaced, fresh[:, HW : 2 * HW], v).astype(jnp.bfloat16)
        kdoc[r] = k
        vdoc[r] = v
        pltpu.make_async_copy(kdoc.at[r], ctx_ref.at[0, place(j)], kout.at[r]).start()
        pltpu.make_async_copy(vdoc.at[r], ctx_ref.at[1, place(j)], vout.at[r]).start()
        for h in heads:
            scores = jnp.dot(k, qt_ref[:, h], preferred_element_type=jnp.float32)
            before = m_ref[:, h]
            top = jnp.maximum(before, jnp.max(scores, axis=0, keepdims=True))
            terms = jnp.exp2((scores - top) * factor)
            fade = jnp.exp2((before - top) * factor)
            m_ref[:, h] = top
            l_ref[:, h] = l_ref[:, h] * fade + jnp.sum(terms, axis=0, keepdims=True)
            acc_ref[:, h] = acc_ref[:, h] * fade + lax.dot_general(
                v,
                terms.astype(jnp.bfloat16),
                (((0,), (0,)), ((), ())),
                preferred_element_type=jnp.float32,
            )
        return 0

    lax.fori_loop(0, count, step, 0)

    if not first:
        live = lax.broadcasted_iota(jnp.int32, (1, SPAN), 1) < count_ref[1]
        for n in range(lanes // SPAN):
            h = slice(n * SPAN, (n + 1) * SPAN)
            mixed = jnp.where(live, acc_ref[:, h] / l_ref[:, h], 0.0)
            out_ref[:, n * HW : (n + 1) * HW] = mixed.T.astype(jnp.bfloat16)

    def finish(r, _):
        pltpu.make_async_copy(kdoc.at[0], ctx_ref.at[0, pl.ds(0, SPAN)], kout.at[r]).wait()
        pltpu.make_async_copy(vdoc.at[0], ctx_ref.at[1, pl.ds(0, SPAN)], vout.at[r]).wait()
        return 0

    lax.fori_loop(0, count, finish, 0)
    if first:
        lax.fori_loop(count_ref[0], MAXDOC, finish, 0)


def attend(first, kbufs, vbufs, table, counts, pos, turns, new, qt, state):
    lanes = qt.shape[1]
    context = jax.ShapeDtypeStruct((2, MAXDOC * SPAN, HW), jnp.bfloat16)
    running = [(1, lanes), (1, lanes), (HW, lanes)]
    if first:
        out_shape = (context, *[jax.ShapeDtypeStruct(s, jnp.float32) for s in running])
        out_specs = (HBM, VMEM, VMEM, VMEM)
    else:
        out_shape = (jax.ShapeDtypeStruct((SPAN, lanes // SPAN * HW), jnp.bfloat16), context)
        out_specs = (VMEM, HBM)
    fixed = 6 + len(kbufs) + len(vbufs)
    documents = MAXDOC // 2
    return pl.pallas_call(
        functools.partial(attend_kernel, first, len(kbufs), len(vbufs)),
        out_shape=out_shape,
        in_specs=[SMEM] * 2
        + [VMEM] * 4
        + ([KEPT] * 14 + [HBM] * (len(kbufs) - 14) if first else [HBM] * len(kbufs))
        + ([KEPT] * 14 + [HBM] * (len(vbufs) - 14) if first else [HBM] * len(vbufs))
        + ([] if first else [VMEM] * 3 + [HBM]),
        out_specs=out_specs,
        scratch_shapes=([] if first else [pltpu.VMEM(s, jnp.float32) for s in running])
        + [pltpu.VMEM((MAXDOC, SPAN, HW), jnp.bfloat16)] * 2
        + [pltpu.VMEM((MAXDOC, 16, HW), jnp.bfloat16)] * 2
        + [pltpu.VMEM((SPAN, HW), jnp.bfloat16)]
        + [pltpu.SemaphoreType.DMA((MAXDOC,))] * 6,
        input_output_aliases={} if first else {fixed + 3: 1},
        compiler_params=pltpu.CompilerParams(vmem_limit_bytes=ROOM),
        cost_estimate=pl.CostEstimate(
            flops=4 * lanes * HW * documents * SPAN,
            bytes_accessed=8 * documents * SPAN * HW,
            transcendentals=lanes * documents * SPAN,
        ),
    )(table, counts, pos, turns, new, qt, *kbufs, *vbufs, *state)


def on_device(
    kv_store,
    kv_scale,
    span_home,
    doc_ids,
    doc_count,
    recompute_rows,
    query_len,
    hidden,
    norm_gain,
    w_q,
    w_kv,
):
    tie = lax.optimization_barrier
    me = lax.axis_index("store")
    my_x, my_z = me // NZ, me % NZ

    scale_rows = jnp.transpose(kv_scale[:, :, 0, :], (1, 0, 2)).reshape(2, -1, 1)
    scale_rows = jnp.pad(scale_rows, ((0, 0), (0, 16 - 2 * STORED), (0, 0)))
    own = jnp.concatenate(
        [
            jnp.transpose(kv_store, (1, 0, 2, 3)).reshape(2, STORED * SPAN, HW),
            jnp.broadcast_to(scale_rows, (2, 16, HW)),
        ],
        axis=1,
    ).reshape(2 * BLOCK, HW)

    def keys_of(a):
        return pack([a], [(0, 0, BLOCK)])

    def values_of(a):
        return pack([a], [(0, BLOCK, BLOCK)])

    def last_hop(a, b, dx, dz):
        left = pack([a], [(0, 0, CUT), (0, 2 * BLOCK - 16, 16)])
        right = pack([b], [(0, CUT, 2 * BLOCK + BLOCK - CUT)])
        return shift(left, dx, dz), shift(right, -dx, -dz)

    z1m, z1p = shift(own, 0, 1), shift(own, 0, -1)
    x1m, x1p = shift(own, 1, 0), shift(own, -1, 0)
    z1m, z1p, x1m, x1p = tie((z1m, z1p, x1m, x1p))
    z2m, z2p = shift(z1m, 0, 1), shift(z1p, 0, -1)
    x2k, x2v = shift(keys_of(x1m), 1, 0), shift(values_of(x1p), -1, 0)
    w0 = pack([x1m, x1p, x2v], [(0, BLOCK, BLOCK), (1, BLOCK, BLOCK), (2, 0, BLOCK)])
    w1m, w1p = shift(w0, 0, 1), shift(w0, 0, -1)
    z3m, z3p = shift(z2m, 0, 1), shift(z2p, 0, -1)
    d1 = pack([z1m, z1p, z2m, z2p], [(n, 0, BLOCK) for n in range(4)])
    d1m, d1p = shift(d1, 1, 0), shift(d1, -1, 0)
    w2m, w2p = shift(w1m, 0, 1), shift(w1p, 0, -1)
    z4k, z4v = shift(keys_of(z3m), 0, 1), shift(values_of(z3p), 0, -1)
    d1a = shift(pack([d1m], [(0, 0, 2 * BLOCK)]), 1, 0)
    d1b = shift(pack([d1p], [(0, 2 * BLOCK, 2 * BLOCK)]), -1, 0)
    d2 = pack([z3m, z3p, z4k], [(n, 0, BLOCK) for n in range(3)])
    d2m, d2p = shift(d2, 1, 0), shift(d2, -1, 0)

    doc_list = doc_ids[0]
    doc_total = doc_count[0]
    span_index = jnp.arange(span_home.shape[0], dtype=jnp.int32)
    position = jnp.sum(
        jnp.where(doc_list[:, None] == span_index[None, :], span_home[None, :], 0), axis=1
    )
    owner, slot = position // STORED, position % STORED
    dx = (owner // NZ - my_x) % NX
    dz = (owner % NZ - my_z) % NZ
    one_x = jnp.where(dx == 3, 0, dx)
    one_z = jnp.where(dz == 4, 6, jnp.where(dz > 4, 14 - 2 * dz, 2 * dz - 1))

    def split(block):
        second = (block == 2) | ((block == 1) & (slot == 2))
        row = block * BLOCK + slot * SPAN
        scale = jnp.where(block == 1, CUT, block * BLOCK + STORED * SPAN)
        scale_second = block * BLOCK + STORED * SPAN - CUT
        return (
            second.astype(jnp.int32),
            jnp.where(second, row - CUT, row),
            jnp.where(second, scale_second, scale),
        )

    live = jnp.arange(MAXDOC) < doc_total
    axis_buf = jnp.where(dx == 0, jnp.where(dz == 0, 0, 3 + one_z), jnp.where(dx == 2, 9, 1 + one_x))
    straight = (dx == 0) | (dz == 0)
    late = (dx != 0) & ((dz == 4) | ((dx == 2) & (one_z >= 4)))
    far = one_z >= 4
    row = slot * SPAN
    key_block = jnp.where(far, one_z - 4, one_z)
    piece, cut_row, cut_scale = split(key_block)
    half = (dx == 2) & ~far & (key_block >= 2)
    kb = jnp.where(far, 15 + one_x, jnp.where(half, 13, 10 + one_x))
    kb = jnp.where(straight, jnp.where((dx == 0) & (dz == 4), 14, axis_buf), kb)
    krow = jnp.where(straight, row, (key_block - 2 * half.astype(jnp.int32)) * BLOCK + row)
    ksc = krow - row + STORED * SPAN
    kb = jnp.where(late, jnp.where(dx == 2, 2 + piece, one_x), kb)
    krow = jnp.where(late & (dx == 2), cut_row, krow)
    ksc = jnp.where(late & (dx == 2), cut_scale, ksc)
    piece, cut_row, cut_scale = split(one_x)
    vb = jnp.where(far, 11 + one_z, 10 + one_z)
    vb = jnp.where(straight, jnp.where((dx == 0) & (dz == 4), 14, axis_buf), vb)
    lone = ((dz == 0) & (dx == 2)) | ((dx == 0) & (dz == 4))
    vrow = jnp.where(straight, jnp.where(lone, row, BLOCK + row), one_x * BLOCK + row)
    vsc = vrow - row + STORED * SPAN
    vb = jnp.where(late, jnp.where(dz == 4, 2 + piece, one_z - 4), vb)
    vrow = jnp.where(late & (dz == 4), cut_row, vrow)
    vsc = jnp.where(late & (dz == 4), cut_scale, vsc)
    facts = jnp.stack([jnp.arange(MAXDOC), slot, kb, krow, ksc, vb, vrow, vsc]).astype(jnp.int32)

    def chosen(flag):
        rank = jnp.sum(jnp.where(jnp.tri(MAXDOC, k=-1, dtype=bool) & flag[None, :], 1, 0), axis=1)
        seat = flag[:, None] & (rank[:, None] == jnp.arange(MAXDOC)[None, :])
        return jnp.sum(jnp.where(seat[None], facts[:, :, None], 0), axis=1)

    early_table, late_table = chosen(live & ~late), chosen(live & late)
    early_count = jnp.sum((live & ~late).astype(jnp.int32))
    counts = jnp.stack([doc_total, query_len[0], early_count, doc_total - early_count]).astype(
        jnp.int32
    )

    shift_cos, shift_sin = rope_angles(jnp.arange(MAXDOC, dtype=jnp.int32) * SPAN, HW)
    turns = jnp.stack(
        [
            jnp.concatenate([shift_cos, shift_cos], axis=1),
            jnp.concatenate([-shift_sin, shift_sin], axis=1),
        ],
        axis=1,
    )

    recompute_total = recompute_rows.shape[1] * recompute_rows.shape[2]
    flat_pos = recompute_rows[0].reshape(recompute_total).astype(jnp.int32)
    query_pos = doc_total * SPAN + jnp.arange(hidden.shape[1] - recompute_total, dtype=jnp.int32)
    row_cos, row_sin = rope_angles(jnp.concatenate([flat_pos, query_pos]), HW)
    layer_input = lax.all_gather(hidden, "tp", axis=2, tiled=True)[0]
    new, qt = project(
        layer_input,
        norm_gain[None],
        w_q,
        w_kv.reshape(w_kv.shape[0], 2 * HW),
        jnp.concatenate([row_cos, row_cos], axis=1),
        jnp.concatenate([-row_sin, row_sin], axis=1),
    )

    w3m, w3p = shift(w2m, 0, 1), shift(w2p, 0, -1)
    w3m, w3p, d2m, d2p, new, qt = tie((w3m, w3p, d2m, d2p, new, qt))
    w4a, w4b = last_hop(w3m, w3p, 0, 1)
    d2a, d2b = last_hop(d2m, d2p, 1, 0)
    straight_bufs = [own, x1m, x1p, z1m, z1p, z2m, z2p, z3m, z3p]
    common = (counts, flat_pos[None], turns, new, qt)
    context, *state = attend(
        True,
        straight_bufs + [x2k, d1m, d1p, d1a, d1b, z4k, d2m, d2p],
        straight_bufs + [x2v, w1m, w1p, w2m, w2p, z4v, w3m, w3p],
        early_table,
        *common,
        [],
    )
    attention, context = attend(
        False,
        [d2m, d2p, d2a, d2b],
        [w3m, w3p, w4a, w4b],
        late_table,
        *common,
        [*state, context],
    )
    return (attention[None], context[None])


def solution(mesh):
    placed = (
        P("store", None, None, "tp"),
        P("store", None, "tp", None),
        P(),
        P("store", None),
        P("store"),
        P("store", None, None),
        P("store"),
        P("store", None, "tp"),
        P(),
        P(None, "tp"),
        P(None, None, "tp"),
    )
    return jax.shard_map(
        on_device,
        mesh=mesh,
        in_specs=placed,
        out_specs=(P("store", None, "tp"), P("store", None, None, "tp")),
        check_vma=False,
    )
```

```python
import functools
import jax
import jax.numpy as jnp
from jax import lax
from jax.experimental import pallas as pl
from jax.experimental.pallas import tpu as pltpu
from jax.sharding import PartitionSpec as P

SPAN = 256
SB = 128
MAXDOC = 20
NX, NZ = 4, 8
HW = 128
LOG2E = 1.4426950408889634
STORED = 3
BLOCK = STORED * SPAN + 16
CUT = BLOCK + 2 * SPAN
ROOM = 20 * 1024 * 1024


rope_base = 500000.0
norm_eps = 1e-05


def rope_angles(positions, head_width):
    halfway = head_width // 2
    exponent = jnp.arange(halfway, dtype=jnp.float32) * (2.0 / head_width)
    inverse_freq = jnp.power(jnp.float32(rope_base), -exponent)
    angles = positions.astype(jnp.float32)[:, None] * inverse_freq[None, :]
    return (jnp.cos(angles), jnp.sin(angles))


def rotate_half(values, cosine, sine_part):
    halfway = values.shape[-1] // 2
    low_half = values[..., :halfway]
    high_half = values[..., halfway:]
    return jnp.concatenate(
        [low_half * cosine - high_half * sine_part, high_half * cosine + low_half * sine_part],
        axis=-1,
    )


def shift(a, dx, dz):
    pairs = [
        (x * NZ + z, ((x + dx) % NX) * NZ + (z + dz) % NZ) for x in range(NX) for z in range(NZ)
    ]
    return lax.ppermute(a, "store", pairs)


HBM = pl.BlockSpec(memory_space=pl.ANY)
KEPT = pl.BlockSpec(memory_space=pltpu.HBM)
VMEM = pl.BlockSpec(memory_space=pltpu.VMEM)
SMEM = pl.BlockSpec(memory_space=pltpu.SMEM)


def pack_kernel(plan, *refs):
    sources, out = refs[:-1], refs[-1]
    at = 0
    for source, start, rows in plan:
        out[at : at + rows] = sources[source][start : start + rows]
        at += rows


def pack(sources, plan):
    rows = sum(p[2] for p in plan)
    return pl.pallas_call(
        functools.partial(pack_kernel, plan),
        out_shape=jax.ShapeDtypeStruct((rows, HW), jnp.bfloat16),
        in_specs=[VMEM] * len(sources),
        out_specs=VMEM,
        compiler_params=pltpu.CompilerParams(vmem_limit_bytes=2 * 1024 * 1024),
        cost_estimate=pl.CostEstimate(
            flops=0, bytes_accessed=4 * rows * HW, transcendentals=0
        ),
    )(*sources)


def halves_kernel(*refs):
    for n in range(0, 4, 2):
        a, b, left, right = refs[n], refs[n + 1], refs[n + 4], refs[n + 5]
        left[:CUT] = a[:CUT]
        left[CUT:] = a[2 * BLOCK - 16 : 2 * BLOCK]
        right[...] = b[CUT:]


def halves(*pairs):
    shapes = [(CUT + 16, HW), (3 * BLOCK - CUT, HW)] * 2
    return pl.pallas_call(
        halves_kernel,
        out_shape=[jax.ShapeDtypeStruct(shape, jnp.bfloat16) for shape in shapes],
        in_specs=[VMEM] * 4,
        out_specs=[VMEM] * 4,
        compiler_params=pltpu.CompilerParams(vmem_limit_bytes=2 * 1024 * 1024),
        cost_estimate=pl.CostEstimate(
            flops=0, bytes_accessed=24 * BLOCK * HW, transcendentals=0
        ),
    )(*pairs)


def project_kernel(hid_ref, gain_ref, wq_ref, wkv_ref, cos_ref, sin_ref, new_ref, qt_ref, nb_ref):
    features = hid_ref.shape[1]
    piece = 512
    total = jnp.zeros((SPAN, 1), jnp.float32)
    for c in range(0, features, piece):
        x = hid_ref[:, c : c + piece].astype(jnp.float32)
        total = total + jnp.sum(x * x, axis=1, keepdims=True)
    inverse = lax.rsqrt(total * (1.0 / features) + norm_eps)
    for c in range(0, features, piece):
        x = hid_ref[:, c : c + piece].astype(jnp.float32)
        gain = gain_ref[:, c : c + piece].astype(jnp.float32)
        nb_ref[:, c : c + piece] = (x * inverse * gain).astype(jnp.bfloat16)
    kv = jnp.dot(nb_ref[...], wkv_ref[...], preferred_element_type=jnp.float32)
    cosine, sine = cos_ref[...], sin_ref[...]
    k = kv[:, :HW]
    new_ref[:, :HW] = (k * cosine + pltpu.roll(k, HW // 2, 1) * sine).astype(jnp.bfloat16)
    new_ref[:, HW : 2 * HW] = kv[:, HW:].astype(jnp.bfloat16)
    new_ref[:, 2 * HW :] = jnp.ones((SPAN, HW), jnp.bfloat16)

    @pl.when(pl.program_id(0) == pl.num_programs(0) - 1)
    def _():
        q = jnp.dot(nb_ref[...], wq_ref[...], preferred_element_type=jnp.float32)
        for h in range(q.shape[1] // HW):
            one = q[:, h * HW : (h + 1) * HW]
            one = one * cosine + pltpu.roll(one, HW // 2, 1) * sine
            qt_ref[:, h * SPAN : (h + 1) * SPAN] = one.T.astype(jnp.bfloat16)


def project(hid, gain, wq, wkv, cosine, sine):
    rows, features = hid.shape
    lanes = wq.shape[1] // HW * SPAN
    return pl.pallas_call(
        project_kernel,
        grid=(rows // SPAN,),
        out_shape=(
            jax.ShapeDtypeStruct((rows, 3 * HW), jnp.bfloat16),
            jax.ShapeDtypeStruct((HW, lanes), jnp.bfloat16),
        ),
        in_specs=[
            pl.BlockSpec((SPAN, features), lambda i: (i, 0)),
            pl.BlockSpec((1, features), lambda i: (0, 0)),
            pl.BlockSpec(wq.shape, lambda i: (0, 0), pipeline_mode=pl.Buffered(1)),
            pl.BlockSpec(wkv.shape, lambda i: (0, 0), pipeline_mode=pl.Buffered(1)),
            pl.BlockSpec((SPAN, HW), lambda i: (i, 0)),
            pl.BlockSpec((SPAN, HW), lambda i: (i, 0)),
        ],
        out_specs=(
            pl.BlockSpec((SPAN, 3 * HW), lambda i: (i, 0)),
            pl.BlockSpec((HW, lanes), lambda i: (0, 0)),
        ),
        scratch_shapes=[pltpu.VMEM((SPAN, features), jnp.bfloat16)],
        compiler_params=pltpu.CompilerParams(vmem_limit_bytes=ROOM),
        cost_estimate=pl.CostEstimate(
            flops=2 * features * HW * (2 * rows + 4 * SPAN),
            bytes_accessed=2 * features * (rows + 6 * HW),
            transcendentals=0,
        ),
    )(hid, gain, wq, wkv, cosine, sine)


DOC, SLOT, KB, KROW, KSC, VB, VROW, VSC = range(8)


def attend_kernel(first, nk, nv, table, count_ref, pos_ref, shift_ref, new_ref, qt_ref, *refs):
    kbufs, vbufs, refs = refs[:nk], refs[nk : nk + nv], refs[nk + nv :]
    if first:
        ctx_ref, m_ref, l_ref, acc_ref = refs[:4]
        refs = refs[4:]
    else:
        m_in, l_in, acc_in, _, out_ref, ctx_ref, m_ref, l_ref, acc_ref = refs[:9]
        refs = refs[9:]
    kdoc, vdoc, kscale, vscale, zero, ksem, vsem, kssem, vssem, kout, vout = refs
    count = count_ref[2] if first else count_ref[3]
    lanes = qt_ref.shape[1]
    nrec = pos_ref.shape[1]
    factor = HW**-0.5 * LOG2E
    heads = [slice(0, lanes)]

    def pick(n, low, high, act):
        if high - low == 1:
            act(low)
            return
        mid = (low + high) // 2

        @pl.when(n < mid)
        def _():
            pick(n, low, mid, act)

        @pl.when(n >= mid)
        def _():
            pick(n, mid, high, act)

    def fetch(r, _):
        def keys(b):
            row = pl.multiple_of(table[KROW, r], 16)
            pltpu.make_async_copy(kbufs[b].at[pl.ds(row, SPAN)], kdoc.at[r], ksem.at[r]).start()
            row = pl.multiple_of(table[KSC, r], 16)
            pltpu.make_async_copy(kbufs[b].at[pl.ds(row, 16)], kscale.at[r], kssem.at[r]).start()

        def values(b):
            row = pl.multiple_of(table[VROW, r], 16)
            pltpu.make_async_copy(vbufs[b].at[pl.ds(row, SPAN)], vdoc.at[r], vsem.at[r]).start()
            row = pl.multiple_of(table[VSC, r], 16)
            pltpu.make_async_copy(vbufs[b].at[pl.ds(row, 16)], vscale.at[r], vssem.at[r]).start()

        pick(table[KB, r], 0, nk, keys)
        pick(table[VB, r], 0, nv, values)
        return 0

    lax.fori_loop(0, count, fetch, 0)

    def place(j):
        return pl.ds(pl.multiple_of(j * SPAN, SPAN), SPAN)

    if first:
        docs = count_ref[0]
        zero[...] = jnp.zeros(zero.shape, zero.dtype)

        def blank(j, _):
            pltpu.make_async_copy(zero, ctx_ref.at[0, place(j)], kout.at[j]).start()
            pltpu.make_async_copy(zero, ctx_ref.at[1, place(j)], vout.at[j]).start()
            return 0

        lax.fori_loop(docs, MAXDOC, blank, 0)

        own_keys = new_ref[nrec:, :HW]
        own_values = new_ref[nrec:, HW : 2 * HW]
        for h in heads:
            scores = jnp.dot(own_keys, qt_ref[:, h], preferred_element_type=jnp.float32)
            key_index = lax.broadcasted_iota(jnp.int32, scores.shape, 0)
            query_index = lax.broadcasted_iota(jnp.int32, scores.shape, 1) & (SPAN - 1)
            scores = jnp.where(key_index <= query_index, scores, -jnp.inf)
            top = jnp.max(scores, axis=0, keepdims=True)
            terms = jnp.exp2((scores - top) * factor)
            m_ref[:, h] = top
            l_ref[:, h] = jnp.sum(terms, axis=0, keepdims=True)
            acc_ref[:, h] = lax.dot_general(
                own_values,
                terms.astype(jnp.bfloat16),
                (((0,), (0,)), ((), ())),
                preferred_element_type=jnp.float32,
            )
    else:
        m_ref[...] = m_in[...]
        l_ref[...] = l_in[...]
        acc_ref[...] = acc_in[...]

    upper = lax.broadcasted_iota(jnp.int32, (SPAN, HW), 0) >= SB
    row_index = lax.broadcasted_iota(jnp.int32, (SPAN, nrec), 0)
    scale_index = lax.broadcasted_iota(jnp.int32, (16, HW), 0)

    def dequant(codes, scales, slot):
        s = scales.astype(jnp.float32)
        low = jnp.sum(jnp.where(scale_index == 2 * slot, s, 0.0), axis=0, keepdims=True)
        high = jnp.sum(jnp.where(scale_index == 2 * slot + 1, s, 0.0), axis=0, keepdims=True)
        return codes.astype(jnp.float32) * jnp.where(upper, high, low)

    def ready(r):
        j, slot = table[DOC, r], table[SLOT, r]
        hit = jnp.where(row_index == pos_ref[...] - j * SPAN, 1.0, 0.0).astype(jnp.bfloat16)
        fresh = jnp.dot(hit, new_ref[:nrec], preferred_element_type=jnp.float32)
        replaced = fresh[:, 2 * HW :] > 0.5
        pltpu.make_async_copy(kbufs[0].at[pl.ds(0, SPAN)], kdoc.at[r], ksem.at[r]).wait()
        pltpu.make_async_copy(kbufs[0].at[pl.ds(0, 16)], kscale.at[r], kssem.at[r]).wait()
        pltpu.make_async_copy(vbufs[0].at[pl.ds(0, SPAN)], vdoc.at[r], vsem.at[r]).wait()
        pltpu.make_async_copy(vbufs[0].at[pl.ds(0, 16)], vscale.at[r], vssem.at[r]).wait()
        k = dequant(kdoc[r], kscale[r], slot)
        turn = shift_ref[j]
        k = k * turn[0:1] + pltpu.roll(k, HW // 2, 1) * turn[1:2]
        k = jnp.where(replaced, fresh[:, :HW], k).astype(jnp.bfloat16)
        v = dequant(vdoc[r], vscale[r], slot)
        v = jnp.where(replaced, fresh[:, HW : 2 * HW], v).astype(jnp.bfloat16)
        kdoc[r] = k
        vdoc[r] = v
        pltpu.make_async_copy(kdoc.at[r], ctx_ref.at[0, place(j)], kout.at[r]).start()
        pltpu.make_async_copy(vdoc.at[r], ctx_ref.at[1, place(j)], vout.at[r]).start()
        return k, v

    def absorb(k, v):
        scores = jnp.dot(k, qt_ref[...], preferred_element_type=jnp.float32)
        before = m_ref[...]
        top = jnp.maximum(before, jnp.max(scores, axis=0, keepdims=True))
        terms = jnp.exp2((scores - top) * factor)
        fade = jnp.exp2((before - top) * factor)
        m_ref[...] = top
        l_ref[...] = l_ref[...] * fade + jnp.sum(terms, axis=0, keepdims=True)
        acc_ref[...] = acc_ref[...] * fade + lax.dot_general(
            v,
            terms.astype(jnp.bfloat16),
            (((0,), (0,)), ((), ())),
            preferred_element_type=jnp.float32,
        )

    def pair(n, _):
        k0, v0 = ready(2 * n)
        k1, v1 = ready(2 * n + 1)
        absorb(jnp.concatenate([k0, k1], axis=0), jnp.concatenate([v0, v1], axis=0))
        return 0

    lax.fori_loop(0, count // 2, pair, 0)

    @pl.when(count % 2 == 1)
    def _():
        absorb(*ready(count - 1))

    if not first:
        live = lax.broadcasted_iota(jnp.int32, (1, SPAN), 1) < count_ref[1]
        for n in range(lanes // SPAN):
            h = slice(n * SPAN, (n + 1) * SPAN)
            mixed = jnp.where(live, acc_ref[:, h] / l_ref[:, h], 0.0)
            out_ref[:, n * HW : (n + 1) * HW] = mixed.T.astype(jnp.bfloat16)

    def finish(r, _):
        pltpu.make_async_copy(kdoc.at[0], ctx_ref.at[0, pl.ds(0, SPAN)], kout.at[r]).wait()
        pltpu.make_async_copy(vdoc.at[0], ctx_ref.at[1, pl.ds(0, SPAN)], vout.at[r]).wait()
        return 0

    lax.fori_loop(0, count, finish, 0)
    if first:
        lax.fori_loop(count_ref[0], MAXDOC, finish, 0)


def attend(first, kbufs, vbufs, table, counts, pos, turns, new, qt, state):
    lanes = qt.shape[1]
    context = jax.ShapeDtypeStruct((2, MAXDOC * SPAN, HW), jnp.bfloat16)
    running = [(1, lanes), (1, lanes), (HW, lanes)]
    if first:
        out_shape = (context, *[jax.ShapeDtypeStruct(s, jnp.float32) for s in running])
        out_specs = (HBM, VMEM, VMEM, VMEM)
    else:
        out_shape = (jax.ShapeDtypeStruct((SPAN, lanes // SPAN * HW), jnp.bfloat16), context)
        out_specs = (VMEM, HBM)
    fixed = 6 + len(kbufs) + len(vbufs)
    documents = MAXDOC // 2
    return pl.pallas_call(
        functools.partial(attend_kernel, first, len(kbufs), len(vbufs)),
        out_shape=out_shape,
        in_specs=[SMEM] * 2
        + [VMEM] * 4
        + [KEPT if first else HBM] * (len(kbufs) + len(vbufs))
        + ([] if first else [VMEM] * 3 + [HBM]),
        out_specs=out_specs,
        scratch_shapes=([] if first else [pltpu.VMEM(s, jnp.float32) for s in running])
        + [pltpu.VMEM((MAXDOC, SPAN, HW), jnp.bfloat16)] * 2
        + [pltpu.VMEM((MAXDOC, 16, HW), jnp.bfloat16)] * 2
        + [pltpu.VMEM((SPAN, HW), jnp.bfloat16)]
        + [pltpu.SemaphoreType.DMA((MAXDOC,))] * 6,
        input_output_aliases={} if first else {fixed + 3: 1},
        compiler_params=pltpu.CompilerParams(vmem_limit_bytes=ROOM),
        cost_estimate=pl.CostEstimate(
            flops=4 * lanes * HW * documents * SPAN,
            bytes_accessed=8 * documents * SPAN * HW,
            transcendentals=lanes * documents * SPAN,
        ),
    )(table, counts, pos, turns, new, qt, *kbufs, *vbufs, *state)


def on_device(
    kv_store,
    kv_scale,
    span_home,
    doc_ids,
    doc_count,
    recompute_rows,
    query_len,
    hidden,
    norm_gain,
    w_q,
    w_kv,
):
    tie = lax.optimization_barrier
    me = lax.axis_index("store")
    my_x, my_z = me // NZ, me % NZ

    scale_rows = jnp.transpose(kv_scale[:, :, 0, :], (1, 0, 2)).reshape(2, -1, 1)
    scale_rows = jnp.pad(scale_rows, ((0, 0), (0, 16 - 2 * STORED), (0, 0)))
    own = jnp.concatenate(
        [
            jnp.transpose(kv_store, (1, 0, 2, 3)).reshape(2, STORED * SPAN, HW),
            jnp.broadcast_to(scale_rows, (2, 16, HW)),
        ],
        axis=1,
    ).reshape(2 * BLOCK, HW)

    def keys_of(a):
        return pack([a], [(0, 0, BLOCK)])

    def values_of(a):
        return pack([a], [(0, BLOCK, BLOCK)])

    z1m, z1p = shift(own, 0, 1), shift(own, 0, -1)
    x1m, x1p = shift(own, 1, 0), shift(own, -1, 0)
    z1m, z1p, x1m, x1p = tie((z1m, z1p, x1m, x1p))
    z2m, z2p = shift(z1m, 0, 1), shift(z1p, 0, -1)
    x2k, x2v = shift(keys_of(x1m), 1, 0), shift(values_of(x1p), -1, 0)
    w0 = pack([x1m, x1p, x2v], [(0, BLOCK, BLOCK), (1, BLOCK, BLOCK), (2, 0, BLOCK)])
    w1m, w1p = shift(w0, 0, 1), shift(w0, 0, -1)
    z3m, z3p = shift(z2m, 0, 1), shift(z2p, 0, -1)
    d1 = pack([z1m, z1p, z2m, z2p], [(n, 0, BLOCK) for n in range(4)])
    d1m, d1p = shift(d1, 1, 0), shift(d1, -1, 0)
    w2m, w2p = shift(w1m, 0, 1), shift(w1p, 0, -1)
    z4k, z4v = shift(keys_of(z3m), 0, 1), shift(values_of(z3p), 0, -1)
    d1a = shift(pack([d1m], [(0, 0, 2 * BLOCK)]), 1, 0)
    d1b = shift(pack([d1p], [(0, 2 * BLOCK, 2 * BLOCK)]), -1, 0)

    doc_list = doc_ids[0]
    doc_total = doc_count[0]
    span_index = jnp.arange(span_home.shape[0], dtype=jnp.int32)
    position = jnp.sum(
        jnp.where(doc_list[:, None] == span_index[None, :], span_home[None, :], 0), axis=1
    )
    owner, slot = position // STORED, position % STORED
    dx = (owner // NZ - my_x) % NX
    dz = (owner % NZ - my_z) % NZ
    one_x = jnp.where(dx == 3, 0, dx)
    one_z = jnp.where(dz == 4, 6, jnp.where(dz > 4, 14 - 2 * dz, 2 * dz - 1))

    def split(block):
        second = (block == 2) | ((block == 1) & (slot == 2))
        row = block * BLOCK + slot * SPAN
        scale = jnp.where(block == 1, CUT, block * BLOCK + STORED * SPAN)
        scale_second = block * BLOCK + STORED * SPAN - CUT
        return (
            second.astype(jnp.int32),
            jnp.where(second, row - CUT, row),
            jnp.where(second, scale_second, scale),
        )

    live = jnp.arange(MAXDOC) < doc_total
    axis_buf = jnp.where(dx == 0, jnp.where(dz == 0, 0, 3 + one_z), jnp.where(dx == 2, 9, 1 + one_x))
    straight = (dx == 0) | (dz == 0)
    late = (dx != 0) & ((dz == 4) | ((dx == 2) & (one_z >= 4)))
    far = one_z >= 4
    row = slot * SPAN
    key_block = jnp.where(far, one_z - 4, one_z)
    piece, cut_row, cut_scale = split(key_block)
    half = (dx == 2) & ~far & (key_block >= 2)
    kb = jnp.where(far, 15 + one_x, jnp.where(half, 13, 10 + one_x))
    kb = jnp.where(straight, jnp.where((dx == 0) & (dz == 4), 14, axis_buf), kb)
    krow = jnp.where(straight, row, (key_block - 2 * half.astype(jnp.int32)) * BLOCK + row)
    ksc = krow - row + STORED * SPAN
    kb = jnp.where(late, jnp.where(dx == 2, 2 + piece, one_x), kb)
    krow = jnp.where(late & (dx == 2), cut_row, krow)
    ksc = jnp.where(late & (dx == 2), cut_scale, ksc)
    piece, cut_row, cut_scale = split(one_x)
    vb = jnp.where(far, 11 + one_z, 10 + one_z)
    vb = jnp.where(straight, jnp.where((dx == 0) & (dz == 4), 14, axis_buf), vb)
    lone = ((dz == 0) & (dx == 2)) | ((dx == 0) & (dz == 4))
    vrow = jnp.where(straight, jnp.where(lone, row, BLOCK + row), one_x * BLOCK + row)
    vsc = vrow - row + STORED * SPAN
    vb = jnp.where(late, jnp.where(dz == 4, 2 + piece, one_z - 4), vb)
    vrow = jnp.where(late & (dz == 4), cut_row, vrow)
    vsc = jnp.where(late & (dz == 4), cut_scale, vsc)
    facts = jnp.stack([jnp.arange(MAXDOC), slot, kb, krow, ksc, vb, vrow, vsc]).astype(jnp.int32)

    def chosen(flag):
        rank = jnp.sum(jnp.where(jnp.tri(MAXDOC, k=-1, dtype=bool) & flag[None, :], 1, 0), axis=1)
        seat = flag[:, None] & (rank[:, None] == jnp.arange(MAXDOC)[None, :])
        return jnp.sum(jnp.where(seat[None], facts[:, :, None], 0), axis=1)

    early_table, late_table = chosen(live & ~late), chosen(live & late)
    early_count = jnp.sum((live & ~late).astype(jnp.int32))
    counts = jnp.stack([doc_total, query_len[0], early_count, doc_total - early_count]).astype(
        jnp.int32
    )

    shift_cos, shift_sin = rope_angles(jnp.arange(MAXDOC, dtype=jnp.int32) * SPAN, HW)
    turns = jnp.stack(
        [
            jnp.concatenate([shift_cos, shift_cos], axis=1),
            jnp.concatenate([-shift_sin, shift_sin], axis=1),
        ],
        axis=1,
    )

    recompute_total = recompute_rows.shape[1] * recompute_rows.shape[2]
    flat_pos = recompute_rows[0].reshape(recompute_total).astype(jnp.int32)
    query_pos = doc_total * SPAN + jnp.arange(hidden.shape[1] - recompute_total, dtype=jnp.int32)
    row_cos, row_sin = rope_angles(jnp.concatenate([flat_pos, query_pos]), HW)
    layer_input = lax.all_gather(hidden, "tp", axis=2, tiled=True)[0]
    new, qt = project(
        layer_input,
        norm_gain[None],
        w_q,
        w_kv.reshape(w_kv.shape[0], 2 * HW),
        jnp.concatenate([row_cos, row_cos], axis=1),
        jnp.concatenate([-row_sin, row_sin], axis=1),
    )

    z4k, new, qt = tie((z4k, new, qt))
    d2 = pack([z3m, z3p, z4k], [(n, 0, BLOCK) for n in range(3)])
    d2m, d2p = shift(d2, 1, 0), shift(d2, -1, 0)
    w3m, w3p = shift(w2m, 0, 1), shift(w2p, 0, -1)
    w3m, w3p, d2m, d2p, new, qt = tie((w3m, w3p, d2m, d2p, new, qt))
    w_left, w_right, d_left, d_right = halves(w3m, w3p, d2m, d2p)
    w4a, w4b = shift(w_left, 0, 1), shift(w_right, 0, -1)
    d2a, d2b = shift(d_left, 1, 0), shift(d_right, -1, 0)
    straight_bufs = [own, x1m, x1p, z1m, z1p, z2m, z2p, z3m, z3p]
    common = (counts, flat_pos[None], turns, new, qt)
    context, *state = attend(
        True,
        straight_bufs + [x2k, d1m, d1p, d1a, d1b, z4k, d2m, d2p],
        straight_bufs + [x2v, w1m, w1p, w2m, w2p, z4v, w3m, w3p],
        early_table,
        *common,
        [],
    )
    attention, context = attend(
        False,
        [d2m, d2p, d2a, d2b],
        [w3m, w3p, w4a, w4b],
        late_table,
        *common,
        [*state, context],
    )
    return (attention[None], context[None])


def solution(mesh):
    placed = (
        P("store", None, None, "tp"),
        P("store", None, "tp", None),
        P(),
        P("store", None),
        P("store"),
        P("store", None, None),
        P("store"),
        P("store", None, "tp"),
        P(),
        P(None, "tp"),
        P(None, None, "tp"),
    )
    return jax.shard_map(
        on_device,
        mesh=mesh,
        in_specs=placed,
        out_specs=(P("store", None, "tp"), P("store", None, None, "tp")),
        check_vma=False,
    )
```

```python
import functools
import jax
import jax.numpy as jnp
from jax import lax
from jax.experimental import pallas as pl
from jax.experimental.pallas import tpu as pltpu
from jax.sharding import PartitionSpec as P

SPAN = 256
SB = 128
MAXDOC = 20
NX, NZ = 4, 8
HW = 128
LOG2E = 1.4426950408889634
STORED = 3
BLOCK = STORED * SPAN + 16
CUT = BLOCK + 2 * SPAN
ROOM = 20 * 1024 * 1024


rope_base = 500000.0
norm_eps = 1e-05


def rope_angles(positions, head_width):
    halfway = head_width // 2
    exponent = jnp.arange(halfway, dtype=jnp.float32) * (2.0 / head_width)
    inverse_freq = jnp.power(jnp.float32(rope_base), -exponent)
    angles = positions.astype(jnp.float32)[:, None] * inverse_freq[None, :]
    return (jnp.cos(angles), jnp.sin(angles))


def rotate_half(values, cosine, sine_part):
    halfway = values.shape[-1] // 2
    low_half = values[..., :halfway]
    high_half = values[..., halfway:]
    return jnp.concatenate(
        [low_half * cosine - high_half * sine_part, high_half * cosine + low_half * sine_part],
        axis=-1,
    )


def shift(a, dx, dz):
    pairs = [
        (x * NZ + z, ((x + dx) % NX) * NZ + (z + dz) % NZ) for x in range(NX) for z in range(NZ)
    ]
    return lax.ppermute(a, "store", pairs)


HBM = pl.BlockSpec(memory_space=pl.ANY)
KEPT = pl.BlockSpec(memory_space=pltpu.HBM)
VMEM = pl.BlockSpec(memory_space=pltpu.VMEM)
SMEM = pl.BlockSpec(memory_space=pltpu.SMEM)


def pack_kernel(plan, *refs):
    sources, out = refs[:-1], refs[-1]
    at = 0
    for source, start, rows in plan:
        out[at : at + rows] = sources[source][start : start + rows]
        at += rows


def pack(sources, plan):
    rows = sum(p[2] for p in plan)
    return pl.pallas_call(
        functools.partial(pack_kernel, plan),
        out_shape=jax.ShapeDtypeStruct((rows, HW), jnp.bfloat16),
        in_specs=[VMEM] * len(sources),
        out_specs=VMEM,
        compiler_params=pltpu.CompilerParams(vmem_limit_bytes=2 * 1024 * 1024),
        cost_estimate=pl.CostEstimate(
            flops=0, bytes_accessed=4 * rows * HW, transcendentals=0
        ),
    )(*sources)


def halves_kernel(*refs):
    for n in range(0, 4, 2):
        a, b, left, right = refs[n], refs[n + 1], refs[n + 4], refs[n + 5]
        left[:CUT] = a[:CUT]
        left[CUT:] = a[2 * BLOCK - 16 : 2 * BLOCK]
        right[...] = b[CUT:]


def halves(*pairs):
    shapes = [(CUT + 16, HW), (3 * BLOCK - CUT, HW)] * 2
    return pl.pallas_call(
        halves_kernel,
        out_shape=[jax.ShapeDtypeStruct(shape, jnp.bfloat16) for shape in shapes],
        in_specs=[VMEM] * 4,
        out_specs=[VMEM] * 4,
        compiler_params=pltpu.CompilerParams(vmem_limit_bytes=2 * 1024 * 1024),
        cost_estimate=pl.CostEstimate(
            flops=0, bytes_accessed=24 * BLOCK * HW, transcendentals=0
        ),
    )(*pairs)


def project_kernel(hid_ref, gain_ref, wq_ref, wkv_ref, cos_ref, sin_ref, new_ref, qt_ref, nb_ref):
    features = hid_ref.shape[1]
    piece = 512
    total = jnp.zeros((SPAN, 1), jnp.float32)
    for c in range(0, features, piece):
        x = hid_ref[:, c : c + piece].astype(jnp.float32)
        total = total + jnp.sum(x * x, axis=1, keepdims=True)
    inverse = lax.rsqrt(total * (1.0 / features) + norm_eps)
    for c in range(0, features, piece):
        x = hid_ref[:, c : c + piece].astype(jnp.float32)
        gain = gain_ref[:, c : c + piece].astype(jnp.float32)
        nb_ref[:, c : c + piece] = (x * inverse * gain).astype(jnp.bfloat16)
    kv = jnp.dot(nb_ref[...], wkv_ref[...], preferred_element_type=jnp.float32)
    cosine, sine = cos_ref[...], sin_ref[...]
    k = kv[:, :HW]
    new_ref[:, :HW] = (k * cosine + pltpu.roll(k, HW // 2, 1) * sine).astype(jnp.bfloat16)
    new_ref[:, HW : 2 * HW] = kv[:, HW:].astype(jnp.bfloat16)
    new_ref[:, 2 * HW :] = jnp.ones((SPAN, HW), jnp.bfloat16)

    @pl.when(pl.program_id(0) == pl.num_programs(0) - 1)
    def _():
        q = jnp.dot(nb_ref[...], wq_ref[...], preferred_element_type=jnp.float32)
        for h in range(q.shape[1] // HW):
            one = q[:, h * HW : (h + 1) * HW]
            one = one * cosine + pltpu.roll(one, HW // 2, 1) * sine
            qt_ref[:, h * SPAN : (h + 1) * SPAN] = one.T.astype(jnp.bfloat16)


def project(hid, gain, wq, wkv, cosine, sine):
    rows, features = hid.shape
    lanes = wq.shape[1] // HW * SPAN
    return pl.pallas_call(
        project_kernel,
        grid=(rows // SPAN,),
        out_shape=(
            jax.ShapeDtypeStruct((rows, 3 * HW), jnp.bfloat16),
            jax.ShapeDtypeStruct((HW, lanes), jnp.bfloat16),
        ),
        in_specs=[
            pl.BlockSpec((SPAN, features), lambda i: (i, 0)),
            pl.BlockSpec((1, features), lambda i: (0, 0)),
            pl.BlockSpec(wq.shape, lambda i: (0, 0), pipeline_mode=pl.Buffered(1)),
            pl.BlockSpec(wkv.shape, lambda i: (0, 0), pipeline_mode=pl.Buffered(1)),
            pl.BlockSpec((SPAN, HW), lambda i: (i, 0)),
            pl.BlockSpec((SPAN, HW), lambda i: (i, 0)),
        ],
        out_specs=(
            pl.BlockSpec((SPAN, 3 * HW), lambda i: (i, 0)),
            pl.BlockSpec((HW, lanes), lambda i: (0, 0)),
        ),
        scratch_shapes=[pltpu.VMEM((SPAN, features), jnp.bfloat16)],
        compiler_params=pltpu.CompilerParams(vmem_limit_bytes=ROOM),
        cost_estimate=pl.CostEstimate(
            flops=2 * features * HW * (2 * rows + 4 * SPAN),
            bytes_accessed=2 * features * (rows + 6 * HW),
            transcendentals=0,
        ),
    )(hid, gain, wq, wkv, cosine, sine)


DOC, SLOT, KB, KROW, KSC, VB, VROW, VSC = range(8)


def attend_kernel(first, nk, nv, table, count_ref, pos_ref, shift_ref, new_ref, qt_ref, *refs):
    kbufs, vbufs, refs = refs[:nk], refs[nk : nk + nv], refs[nk + nv :]
    if first:
        ctx_ref, m_ref, l_ref, acc_ref = refs[:4]
        refs = refs[4:]
    else:
        m_in, l_in, acc_in, _, out_ref, ctx_ref, m_ref, l_ref, acc_ref = refs[:9]
        refs = refs[9:]
    kdoc, vdoc, kscale, vscale, zero, ksem, vsem, kssem, vssem, kout, vout = refs
    count = count_ref[2] if first else count_ref[3]
    lanes = qt_ref.shape[1]
    nrec = pos_ref.shape[1]
    factor = HW**-0.5 * LOG2E
    heads = [slice(0, lanes)]

    def pick(n, low, high, act):
        if high - low == 1:
            act(low)
            return
        mid = (low + high) // 2

        @pl.when(n < mid)
        def _():
            pick(n, low, mid, act)

        @pl.when(n >= mid)
        def _():
            pick(n, mid, high, act)

    def fetch(r, _):
        def keys(b):
            row = pl.multiple_of(table[KROW, r], 16)
            pltpu.make_async_copy(kbufs[b].at[pl.ds(row, SPAN)], kdoc.at[r], ksem.at[r]).start()
            row = pl.multiple_of(table[KSC, r], 16)
            pltpu.make_async_copy(kbufs[b].at[pl.ds(row, 16)], kscale.at[r], kssem.at[r]).start()

        def values(b):
            row = pl.multiple_of(table[VROW, r], 16)
            pltpu.make_async_copy(vbufs[b].at[pl.ds(row, SPAN)], vdoc.at[r], vsem.at[r]).start()
            row = pl.multiple_of(table[VSC, r], 16)
            pltpu.make_async_copy(vbufs[b].at[pl.ds(row, 16)], vscale.at[r], vssem.at[r]).start()

        pick(table[KB, r], 0, nk, keys)
        pick(table[VB, r], 0, nv, values)
        return 0

    lax.fori_loop(0, count, fetch, 0)

    def place(j):
        return pl.ds(pl.multiple_of(j * SPAN, SPAN), SPAN)

    if first:
        docs = count_ref[0]
        zero[...] = jnp.zeros(zero.shape, zero.dtype)

        def blank(j, _):
            pltpu.make_async_copy(zero, ctx_ref.at[0, place(j)], kout.at[j]).start()
            pltpu.make_async_copy(zero, ctx_ref.at[1, place(j)], vout.at[j]).start()
            return 0

        lax.fori_loop(docs, MAXDOC, blank, 0)

        own_keys = new_ref[nrec:, :HW]
        own_values = new_ref[nrec:, HW : 2 * HW]
        for h in heads:
            scores = jnp.dot(own_keys, qt_ref[:, h], preferred_element_type=jnp.float32)
            key_index = lax.broadcasted_iota(jnp.int32, scores.shape, 0)
            query_index = lax.broadcasted_iota(jnp.int32, scores.shape, 1) & (SPAN - 1)
            scores = jnp.where(key_index <= query_index, scores, -jnp.inf)
            top = jnp.max(scores, axis=0, keepdims=True)
            terms = jnp.exp2((scores - top) * factor)
            m_ref[:, h] = top
            l_ref[:, h] = jnp.sum(terms, axis=0, keepdims=True)
            acc_ref[:, h] = lax.dot_general(
                own_values,
                terms.astype(jnp.bfloat16),
                (((0,), (0,)), ((), ())),
                preferred_element_type=jnp.float32,
            )
    else:
        m_ref[...] = m_in[...]
        l_ref[...] = l_in[...]
        acc_ref[...] = acc_in[...]

    upper = lax.broadcasted_iota(jnp.int32, (SPAN, HW), 0) >= SB
    row_index = lax.broadcasted_iota(jnp.int32, (SPAN, nrec), 0)
    scale_index = lax.broadcasted_iota(jnp.int32, (16, HW), 0)

    def dequant(codes, scales, slot):
        s = scales.astype(jnp.float32)
        low = jnp.sum(jnp.where(scale_index == 2 * slot, s, 0.0), axis=0, keepdims=True)
        high = jnp.sum(jnp.where(scale_index == 2 * slot + 1, s, 0.0), axis=0, keepdims=True)
        return codes.astype(jnp.float32) * jnp.where(upper, high, low)

    def ready(r):
        j, slot = table[DOC, r], table[SLOT, r]
        hit = jnp.where(row_index == pos_ref[...] - j * SPAN, 1.0, 0.0).astype(jnp.bfloat16)
        fresh = jnp.dot(hit, new_ref[:nrec], preferred_element_type=jnp.float32)
        replaced = fresh[:, 2 * HW :] > 0.5
        pltpu.make_async_copy(kbufs[0].at[pl.ds(0, SPAN)], kdoc.at[r], ksem.at[r]).wait()
        pltpu.make_async_copy(kbufs[0].at[pl.ds(0, 16)], kscale.at[r], kssem.at[r]).wait()
        pltpu.make_async_copy(vbufs[0].at[pl.ds(0, SPAN)], vdoc.at[r], vsem.at[r]).wait()
        pltpu.make_async_copy(vbufs[0].at[pl.ds(0, 16)], vscale.at[r], vssem.at[r]).wait()
        k = dequant(kdoc[r], kscale[r], slot)
        turn = shift_ref[j]
        k = k * turn[0:1] + pltpu.roll(k, HW // 2, 1) * turn[1:2]
        k = jnp.where(replaced, fresh[:, :HW], k).astype(jnp.bfloat16)
        v = dequant(vdoc[r], vscale[r], slot)
        v = jnp.where(replaced, fresh[:, HW : 2 * HW], v).astype(jnp.bfloat16)
        kdoc[r] = k
        vdoc[r] = v
        pltpu.make_async_copy(kdoc.at[r], ctx_ref.at[0, place(j)], kout.at[r]).start()
        pltpu.make_async_copy(vdoc.at[r], ctx_ref.at[1, place(j)], vout.at[r]).start()
        return k, v

    def absorb(k, v):
        scores = jnp.dot(k, qt_ref[...], preferred_element_type=jnp.float32)
        before = m_ref[...]
        top = jnp.maximum(before, jnp.max(scores, axis=0, keepdims=True))
        terms = jnp.exp2((scores - top) * factor)
        fade = jnp.exp2((before - top) * factor)
        m_ref[...] = top
        l_ref[...] = l_ref[...] * fade + jnp.sum(terms, axis=0, keepdims=True)
        acc_ref[...] = acc_ref[...] * fade + lax.dot_general(
            v,
            terms.astype(jnp.bfloat16),
            (((0,), (0,)), ((), ())),
            preferred_element_type=jnp.float32,
        )

    def pair(n, _):
        k0, v0 = ready(2 * n)
        k1, v1 = ready(2 * n + 1)
        absorb(jnp.concatenate([k0, k1], axis=0), jnp.concatenate([v0, v1], axis=0))
        return 0

    lax.fori_loop(0, count // 2, pair, 0)

    @pl.when(count % 2 == 1)
    def _():
        absorb(*ready(count - 1))

    if not first:
        live = lax.broadcasted_iota(jnp.int32, (1, SPAN), 1) < count_ref[1]
        for n in range(lanes // SPAN):
            h = slice(n * SPAN, (n + 1) * SPAN)
            mixed = jnp.where(live, acc_ref[:, h] / l_ref[:, h], 0.0)
            out_ref[:, n * HW : (n + 1) * HW] = mixed.T.astype(jnp.bfloat16)

    def finish(r, _):
        pltpu.make_async_copy(kdoc.at[0], ctx_ref.at[0, pl.ds(0, SPAN)], kout.at[r]).wait()
        pltpu.make_async_copy(vdoc.at[0], ctx_ref.at[1, pl.ds(0, SPAN)], vout.at[r]).wait()
        return 0

    lax.fori_loop(0, count, finish, 0)
    if first:
        lax.fori_loop(count_ref[0], MAXDOC, finish, 0)


def attend(first, kbufs, vbufs, table, counts, pos, turns, new, qt, state):
    lanes = qt.shape[1]
    context = jax.ShapeDtypeStruct((2, MAXDOC * SPAN, HW), jnp.bfloat16)
    running = [(1, lanes), (1, lanes), (HW, lanes)]
    if first:
        out_shape = (context, *[jax.ShapeDtypeStruct(s, jnp.float32) for s in running])
        out_specs = (HBM, VMEM, VMEM, VMEM)
    else:
        out_shape = (jax.ShapeDtypeStruct((SPAN, lanes // SPAN * HW), jnp.bfloat16), context)
        out_specs = (VMEM, HBM)
    fixed = 6 + len(kbufs) + len(vbufs)
    documents = MAXDOC // 2
    return pl.pallas_call(
        functools.partial(attend_kernel, first, len(kbufs), len(vbufs)),
        out_shape=out_shape,
        in_specs=[SMEM] * 2
        + [VMEM] * 4
        + [KEPT if first else HBM] * (len(kbufs) + len(vbufs))
        + ([] if first else [VMEM] * 3 + [HBM]),
        out_specs=out_specs,
        scratch_shapes=([] if first else [pltpu.VMEM(s, jnp.float32) for s in running])
        + [pltpu.VMEM((MAXDOC, SPAN, HW), jnp.bfloat16)] * 2
        + [pltpu.VMEM((MAXDOC, 16, HW), jnp.bfloat16)] * 2
        + [pltpu.VMEM((SPAN, HW), jnp.bfloat16)]
        + [pltpu.SemaphoreType.DMA((MAXDOC,))] * 6,
        input_output_aliases={} if first else {fixed + 3: 1},
        compiler_params=pltpu.CompilerParams(vmem_limit_bytes=ROOM),
        cost_estimate=pl.CostEstimate(
            flops=4 * lanes * HW * documents * SPAN,
            bytes_accessed=8 * documents * SPAN * HW,
            transcendentals=lanes * documents * SPAN,
        ),
    )(table, counts, pos, turns, new, qt, *kbufs, *vbufs, *state)


def on_device(
    kv_store,
    kv_scale,
    span_home,
    doc_ids,
    doc_count,
    recompute_rows,
    query_len,
    hidden,
    norm_gain,
    w_q,
    w_kv,
):
    tie = lax.optimization_barrier
    me = lax.axis_index("store")
    my_x, my_z = me // NZ, me % NZ

    scale_rows = jnp.transpose(kv_scale[:, :, 0, :], (1, 0, 2)).reshape(2, -1, 1)
    scale_rows = jnp.pad(scale_rows, ((0, 0), (0, 16 - 2 * STORED), (0, 0)))
    own = jnp.concatenate(
        [
            jnp.transpose(kv_store, (1, 0, 2, 3)).reshape(2, STORED * SPAN, HW),
            jnp.broadcast_to(scale_rows, (2, 16, HW)),
        ],
        axis=1,
    ).reshape(2 * BLOCK, HW)

    def keys_of(a):
        return pack([a], [(0, 0, BLOCK)])

    def values_of(a):
        return pack([a], [(0, BLOCK, BLOCK)])

    z1m, z1p = shift(own, 0, 1), shift(own, 0, -1)
    x1m, x1p = shift(own, 1, 0), shift(own, -1, 0)

    doc_list = doc_ids[0]
    doc_total = doc_count[0]
    span_index = jnp.arange(span_home.shape[0], dtype=jnp.int32)
    position = jnp.sum(
        jnp.where(doc_list[:, None] == span_index[None, :], span_home[None, :], 0), axis=1
    )
    owner, slot = position // STORED, position % STORED
    dx = (owner // NZ - my_x) % NX
    dz = (owner % NZ - my_z) % NZ
    one_x = jnp.where(dx == 3, 0, dx)
    one_z = jnp.where(dz == 4, 6, jnp.where(dz > 4, 14 - 2 * dz, 2 * dz - 1))

    def split(block):
        second = (block == 2) | ((block == 1) & (slot == 2))
        row = block * BLOCK + slot * SPAN
        scale = jnp.where(block == 1, CUT, block * BLOCK + STORED * SPAN)
        scale_second = block * BLOCK + STORED * SPAN - CUT
        return (
            second.astype(jnp.int32),
            jnp.where(second, row - CUT, row),
            jnp.where(second, scale_second, scale),
        )

    live = jnp.arange(MAXDOC) < doc_total
    axis_buf = jnp.where(dx == 0, jnp.where(dz == 0, 0, 3 + one_z), jnp.where(dx == 2, 9, 1 + one_x))
    straight = (dx == 0) | (dz == 0)
    late = (dx != 0) & ((dz == 4) | ((dx == 2) & (one_z >= 4)))
    far = one_z >= 4
    row = slot * SPAN
    key_block = jnp.where(far, one_z - 4, one_z)
    piece, cut_row, cut_scale = split(key_block)
    half = (dx == 2) & ~far & (key_block >= 2)
    kb = jnp.where(far, 15 + one_x, jnp.where(half, 13, 10 + one_x))
    kb = jnp.where(straight, jnp.where((dx == 0) & (dz == 4), 14, axis_buf), kb)
    krow = jnp.where(straight, row, (key_block - 2 * half.astype(jnp.int32)) * BLOCK + row)
    ksc = krow - row + STORED * SPAN
    kb = jnp.where(late, jnp.where(dx == 2, 2 + piece, one_x), kb)
    krow = jnp.where(late & (dx == 2), cut_row, krow)
    ksc = jnp.where(late & (dx == 2), cut_scale, ksc)
    piece, cut_row, cut_scale = split(one_x)
    vb = jnp.where(far, 11 + one_z, 10 + one_z)
    vb = jnp.where(straight, jnp.where((dx == 0) & (dz == 4), 14, axis_buf), vb)
    lone = ((dz == 0) & (dx == 2)) | ((dx == 0) & (dz == 4))
    vrow = jnp.where(straight, jnp.where(lone, row, BLOCK + row), one_x * BLOCK + row)
    vsc = vrow - row + STORED * SPAN
    vb = jnp.where(late, jnp.where(dz == 4, 2 + piece, one_z - 4), vb)
    vrow = jnp.where(late & (dz == 4), cut_row, vrow)
    vsc = jnp.where(late & (dz == 4), cut_scale, vsc)
    facts = jnp.stack([jnp.arange(MAXDOC), slot, kb, krow, ksc, vb, vrow, vsc]).astype(jnp.int32)

    def chosen(flag):
        rank = jnp.sum(jnp.where(jnp.tri(MAXDOC, k=-1, dtype=bool) & flag[None, :], 1, 0), axis=1)
        seat = flag[:, None] & (rank[:, None] == jnp.arange(MAXDOC)[None, :])
        return jnp.sum(jnp.where(seat[None], facts[:, :, None], 0), axis=1)

    early_table, late_table = chosen(live & ~late), chosen(live & late)
    early_count = jnp.sum((live & ~late).astype(jnp.int32))
    counts = jnp.stack([doc_total, query_len[0], early_count, doc_total - early_count]).astype(
        jnp.int32
    )

    shift_cos, shift_sin = rope_angles(jnp.arange(MAXDOC, dtype=jnp.int32) * SPAN, HW)
    turns = jnp.stack(
        [
            jnp.concatenate([shift_cos, shift_cos], axis=1),
            jnp.concatenate([-shift_sin, shift_sin], axis=1),
        ],
        axis=1,
    )

    recompute_total = recompute_rows.shape[1] * recompute_rows.shape[2]
    flat_pos = recompute_rows[0].reshape(recompute_total).astype(jnp.int32)
    query_pos = doc_total * SPAN + jnp.arange(hidden.shape[1] - recompute_total, dtype=jnp.int32)
    row_cos, row_sin = rope_angles(jnp.concatenate([flat_pos, query_pos]), HW)
    layer_input = lax.all_gather(hidden, "tp", axis=2, tiled=True)[0]
    small = (
        norm_gain[None],
        w_kv.reshape(w_kv.shape[0], 2 * HW),
        jnp.concatenate([row_cos, row_cos], axis=1),
        jnp.concatenate([-row_sin, row_sin], axis=1),
        early_table,
        late_table,
        counts,
        flat_pos[None],
        turns,
    )
    z1m, z1p, x1m, x1p, small = tie((z1m, z1p, x1m, x1p, small))
    gain, w_kv, cosine, sine, early_table, late_table, counts, pos, turns = small

    z2m, z2p = shift(z1m, 0, 1), shift(z1p, 0, -1)
    x2k, x2v = shift(keys_of(x1m), 1, 0), shift(values_of(x1p), -1, 0)
    w0 = pack([x1m, x1p, x2v], [(0, BLOCK, BLOCK), (1, BLOCK, BLOCK), (2, 0, BLOCK)])
    w1m, w1p = shift(w0, 0, 1), shift(w0, 0, -1)
    z3m, z3p = shift(z2m, 0, 1), shift(z2p, 0, -1)
    d1 = pack([z1m, z1p, z2m, z2p], [(n, 0, BLOCK) for n in range(4)])
    d1m, d1p = shift(d1, 1, 0), shift(d1, -1, 0)
    w2m, w2p = shift(w1m, 0, 1), shift(w1p, 0, -1)
    d1a = shift(pack([d1m], [(0, 0, 2 * BLOCK)]), 1, 0)
    d1b = shift(pack([d1p], [(0, 2 * BLOCK, 2 * BLOCK)]), -1, 0)
    new, qt = project(layer_input, gain, w_q, w_kv, cosine, sine)
    z3m, z3p, new, qt = tie((z3m, z3p, new, qt))
    z4k, z4v = shift(keys_of(z3m), 0, 1), shift(values_of(z3p), 0, -1)
    d2 = pack([z3m, z3p, z4k], [(n, 0, BLOCK) for n in range(3)])
    d2m, d2p = shift(d2, 1, 0), shift(d2, -1, 0)
    w3m, w3p = shift(w2m, 0, 1), shift(w2p, 0, -1)
    w3m, w3p, d2m, d2p, new, qt = tie((w3m, w3p, d2m, d2p, new, qt))
    w_left, w_right, d_left, d_right = halves(w3m, w3p, d2m, d2p)
    w4a, w4b = shift(w_left, 0, 1), shift(w_right, 0, -1)
    d2a, d2b = shift(d_left, 1, 0), shift(d_right, -1, 0)
    straight_bufs = [own, x1m, x1p, z1m, z1p, z2m, z2p, z3m, z3p]
    common = (counts, pos, turns, new, qt)
    context, *state = attend(
        True,
        straight_bufs + [x2k, d1m, d1p, d1a, d1b, z4k, d2m, d2p],
        straight_bufs + [x2v, w1m, w1p, w2m, w2p, z4v, w3m, w3p],
        early_table,
        *common,
        [],
    )
    attention, context = attend(
        False,
        [d2m, d2p, d2a, d2b],
        [w3m, w3p, w4a, w4b],
        late_table,
        *common,
        [*state, context],
    )
    return (attention[None], context[None])


def solution(mesh):
    placed = (
        P("store", None, None, "tp"),
        P("store", None, "tp", None),
        P(),
        P("store", None),
        P("store"),
        P("store", None, None),
        P("store"),
        P("store", None, "tp"),
        P(),
        P(None, "tp"),
        P(None, None, "tp"),
    )
    return jax.shard_map(
        on_device,
        mesh=mesh,
        in_specs=placed,
        out_specs=(P("store", None, "tp"), P("store", None, None, "tp")),
        check_vma=False,
    )
```

```python
import functools
import jax
import jax.numpy as jnp
from jax import lax
from jax.experimental import pallas as pl
from jax.experimental.pallas import tpu as pltpu
from jax.sharding import PartitionSpec as P

SPAN = 256
SB = 128
MAXDOC = 20
NX, NZ = 4, 8
HW = 128
LOG2E = 1.4426950408889634
STORED = 3
BLOCK = STORED * SPAN + 16
CUT = BLOCK + 2 * SPAN
ROOM = 20 * 1024 * 1024


rope_base = 500000.0
norm_eps = 1e-05


def rope_angles(positions, head_width):
    halfway = head_width // 2
    exponent = jnp.arange(halfway, dtype=jnp.float32) * (2.0 / head_width)
    inverse_freq = jnp.power(jnp.float32(rope_base), -exponent)
    angles = positions.astype(jnp.float32)[:, None] * inverse_freq[None, :]
    return (jnp.cos(angles), jnp.sin(angles))


def rotate_half(values, cosine, sine_part):
    halfway = values.shape[-1] // 2
    low_half = values[..., :halfway]
    high_half = values[..., halfway:]
    return jnp.concatenate(
        [low_half * cosine - high_half * sine_part, high_half * cosine + low_half * sine_part],
        axis=-1,
    )


def shift(a, dx, dz):
    pairs = [
        (x * NZ + z, ((x + dx) % NX) * NZ + (z + dz) % NZ) for x in range(NX) for z in range(NZ)
    ]
    return lax.ppermute(a, "store", pairs)


HBM = pl.BlockSpec(memory_space=pl.ANY)
KEPT = pl.BlockSpec(memory_space=pltpu.HBM)
VMEM = pl.BlockSpec(memory_space=pltpu.VMEM)
SMEM = pl.BlockSpec(memory_space=pltpu.SMEM)


def pack_kernel(plan, *refs):
    sources, out = refs[:-1], refs[-1]
    at = 0
    for source, start, rows in plan:
        out[at : at + rows] = sources[source][start : start + rows]
        at += rows


def pack(sources, plan):
    rows = sum(p[2] for p in plan)
    return pl.pallas_call(
        functools.partial(pack_kernel, plan),
        out_shape=jax.ShapeDtypeStruct((rows, HW), jnp.bfloat16),
        in_specs=[VMEM] * len(sources),
        out_specs=VMEM,
        compiler_params=pltpu.CompilerParams(vmem_limit_bytes=6 * 1024 * 1024),
        cost_estimate=pl.CostEstimate(
            flops=0, bytes_accessed=4 * rows * HW, transcendentals=0
        ),
    )(*sources)


def halves_kernel(*refs):
    for n in range(0, 4, 2):
        a, b, left, right = refs[n], refs[n + 1], refs[n + 4], refs[n + 5]
        left[:CUT] = a[:CUT]
        left[CUT:] = a[2 * BLOCK - 16 : 2 * BLOCK]
        right[...] = b[CUT:]


def halves(*pairs):
    shapes = [(CUT + 16, HW), (3 * BLOCK - CUT, HW)] * 2
    return pl.pallas_call(
        halves_kernel,
        out_shape=[jax.ShapeDtypeStruct(shape, jnp.bfloat16) for shape in shapes],
        in_specs=[VMEM] * 4,
        out_specs=[VMEM] * 4,
        compiler_params=pltpu.CompilerParams(vmem_limit_bytes=6 * 1024 * 1024),
        cost_estimate=pl.CostEstimate(
            flops=0, bytes_accessed=24 * BLOCK * HW, transcendentals=0
        ),
    )(*pairs)


def project_kernel(hid_ref, gain_ref, wq_ref, wkv_ref, angle_ref, new_ref, qt_ref, nb_ref):
    features = hid_ref.shape[1]
    piece = 512
    total = jnp.zeros((SPAN, 1), jnp.float32)
    for c in range(0, features, piece):
        x = hid_ref[:, c : c + piece].astype(jnp.float32)
        total = total + jnp.sum(x * x, axis=1, keepdims=True)
    inverse = lax.rsqrt(total * (1.0 / features) + norm_eps)
    for c in range(0, features, piece):
        x = hid_ref[:, c : c + piece].astype(jnp.float32)
        gain = gain_ref[:, c : c + piece].astype(jnp.float32)
        nb_ref[:, c : c + piece] = (x * inverse * gain).astype(jnp.bfloat16)
    kv = jnp.dot(nb_ref[...], wkv_ref[...], preferred_element_type=jnp.float32)
    angles = angle_ref[...]
    swapped = pltpu.roll(angles, HW // 2, 1)
    low = lax.broadcasted_iota(jnp.int32, angles.shape, 1) < HW // 2
    cosine = jnp.where(low, angles, swapped)
    sine = jnp.where(low, -swapped, angles)
    k = kv[:, :HW]
    new_ref[:, :HW] = (k * cosine + pltpu.roll(k, HW // 2, 1) * sine).astype(jnp.bfloat16)
    new_ref[:, HW : 2 * HW] = kv[:, HW:].astype(jnp.bfloat16)
    new_ref[:, 2 * HW :] = jnp.ones((SPAN, HW), jnp.bfloat16)

    @pl.when(pl.program_id(0) == pl.num_programs(0) - 1)
    def _():
        q = jnp.dot(nb_ref[...], wq_ref[...], preferred_element_type=jnp.float32)
        for h in range(q.shape[1] // HW):
            one = q[:, h * HW : (h + 1) * HW]
            one = one * cosine + pltpu.roll(one, HW // 2, 1) * sine
            qt_ref[:, h * SPAN : (h + 1) * SPAN] = one.T.astype(jnp.bfloat16)


def project(hid, gain, wq, wkv, angles):
    rows, features = hid.shape
    lanes = wq.shape[1] // HW * SPAN
    return pl.pallas_call(
        project_kernel,
        grid=(rows // SPAN,),
        out_shape=(
            jax.ShapeDtypeStruct((rows, 3 * HW), jnp.bfloat16),
            jax.ShapeDtypeStruct((HW, lanes), jnp.bfloat16),
        ),
        in_specs=[
            pl.BlockSpec((SPAN, features), lambda i: (i, 0)),
            pl.BlockSpec((1, features), lambda i: (0, 0)),
            pl.BlockSpec(wq.shape, lambda i: (0, 0), pipeline_mode=pl.Buffered(1)),
            pl.BlockSpec(wkv.shape, lambda i: (0, 0), pipeline_mode=pl.Buffered(1)),
            pl.BlockSpec((SPAN, HW), lambda i: (i, 0)),
        ],
        out_specs=(
            pl.BlockSpec((SPAN, 3 * HW), lambda i: (i, 0)),
            pl.BlockSpec((HW, lanes), lambda i: (0, 0)),
        ),
        scratch_shapes=[pltpu.VMEM((SPAN, features), jnp.bfloat16)],
        compiler_params=pltpu.CompilerParams(vmem_limit_bytes=ROOM),
        cost_estimate=pl.CostEstimate(
            flops=2 * features * HW * (2 * rows + 4 * SPAN),
            bytes_accessed=2 * features * (rows + 6 * HW),
            transcendentals=0,
        ),
    )(hid, gain, wq, wkv, angles)


DOC, SLOT, KB, KROW, KSC, VB, VROW, VSC = range(8)


def attend_kernel(first, nk, nv, table, count_ref, pos_ref, shift_ref, new_ref, qt_ref, *refs):
    kbufs, vbufs, refs = refs[:nk], refs[nk : nk + nv], refs[nk + nv :]
    if first:
        ctx_ref, m_ref, l_ref, acc_ref = refs[:4]
        refs = refs[4:]
    else:
        m_in, l_in, acc_in, _, out_ref, ctx_ref, m_ref, l_ref, acc_ref = refs[:9]
        refs = refs[9:]
    kdoc, vdoc, kscale, vscale, zero, ksem, vsem, kssem, vssem, kout, vout = refs
    count = count_ref[2] if first else count_ref[3]
    lanes = qt_ref.shape[1]
    nrec = pos_ref.shape[1]
    factor = HW**-0.5 * LOG2E
    heads = [slice(0, lanes)]

    def pick(n, low, high, act):
        if high - low == 1:
            act(low)
            return
        mid = (low + high) // 2

        @pl.when(n < mid)
        def _():
            pick(n, low, mid, act)

        @pl.when(n >= mid)
        def _():
            pick(n, mid, high, act)

    def fetch(r, _):
        def keys(b):
            row = pl.multiple_of(table[KROW, r], 16)
            pltpu.make_async_copy(kbufs[b].at[pl.ds(row, SPAN)], kdoc.at[r], ksem.at[r]).start()
            row = pl.multiple_of(table[KSC, r], 16)
            pltpu.make_async_copy(kbufs[b].at[pl.ds(row, 16)], kscale.at[r], kssem.at[r]).start()

        def values(b):
            row = pl.multiple_of(table[VROW, r], 16)
            pltpu.make_async_copy(vbufs[b].at[pl.ds(row, SPAN)], vdoc.at[r], vsem.at[r]).start()
            row = pl.multiple_of(table[VSC, r], 16)
            pltpu.make_async_copy(vbufs[b].at[pl.ds(row, 16)], vscale.at[r], vssem.at[r]).start()

        pick(table[KB, r], 0, nk, keys)
        pick(table[VB, r], 0, nv, values)
        return 0

    lax.fori_loop(0, count, fetch, 0)

    def place(j):
        return pl.ds(pl.multiple_of(j * SPAN, SPAN), SPAN)

    if first:
        docs = count_ref[0]
        zero[...] = jnp.zeros(zero.shape, zero.dtype)

        def blank(j, _):
            pltpu.make_async_copy(zero, ctx_ref.at[0, place(j)], kout.at[j]).start()
            pltpu.make_async_copy(zero, ctx_ref.at[1, place(j)], vout.at[j]).start()
            return 0

        lax.fori_loop(docs, MAXDOC, blank, 0)

        own_keys = new_ref[nrec:, :HW]
        own_values = new_ref[nrec:, HW : 2 * HW]
        for h in heads:
            scores = jnp.dot(own_keys, qt_ref[:, h], preferred_element_type=jnp.float32)
            key_index = lax.broadcasted_iota(jnp.int32, scores.shape, 0)
            query_index = lax.broadcasted_iota(jnp.int32, scores.shape, 1) & (SPAN - 1)
            scores = jnp.where(key_index <= query_index, scores, -jnp.inf)
            top = jnp.max(scores, axis=0, keepdims=True)
            terms = jnp.exp2((scores - top) * factor)
            m_ref[:, h] = top
            l_ref[:, h] = jnp.sum(terms, axis=0, keepdims=True)
            acc_ref[:, h] = lax.dot_general(
                own_values,
                terms.astype(jnp.bfloat16),
                (((0,), (0,)), ((), ())),
                preferred_element_type=jnp.float32,
            )
    else:
        m_ref[...] = m_in[...]
        l_ref[...] = l_in[...]
        acc_ref[...] = acc_in[...]

    upper = lax.broadcasted_iota(jnp.int32, (SPAN, HW), 0) >= SB
    row_index = lax.broadcasted_iota(jnp.int32, (SPAN, nrec), 0)
    scale_index = lax.broadcasted_iota(jnp.int32, (16, HW), 0)

    def dequant(codes, scales, slot):
        s = scales.astype(jnp.float32)
        low = jnp.sum(jnp.where(scale_index == 2 * slot, s, 0.0), axis=0, keepdims=True)
        high = jnp.sum(jnp.where(scale_index == 2 * slot + 1, s, 0.0), axis=0, keepdims=True)
        return codes.astype(jnp.float32) * jnp.where(upper, high, low)

    def ready(r):
        j, slot = table[DOC, r], table[SLOT, r]
        hit = jnp.where(row_index == pos_ref[...] - j * SPAN, 1.0, 0.0).astype(jnp.bfloat16)
        fresh = jnp.dot(hit, new_ref[:nrec], preferred_element_type=jnp.float32)
        replaced = fresh[:, 2 * HW :] > 0.5
        pltpu.make_async_copy(kbufs[0].at[pl.ds(0, SPAN)], kdoc.at[r], ksem.at[r]).wait()
        pltpu.make_async_copy(kbufs[0].at[pl.ds(0, 16)], kscale.at[r], kssem.at[r]).wait()
        pltpu.make_async_copy(vbufs[0].at[pl.ds(0, SPAN)], vdoc.at[r], vsem.at[r]).wait()
        pltpu.make_async_copy(vbufs[0].at[pl.ds(0, 16)], vscale.at[r], vssem.at[r]).wait()
        k = dequant(kdoc[r], kscale[r], slot)
        turn = shift_ref[j]
        k = k * turn[0:1] + pltpu.roll(k, HW // 2, 1) * turn[1:2]
        k = jnp.where(replaced, fresh[:, :HW], k).astype(jnp.bfloat16)
        v = dequant(vdoc[r], vscale[r], slot)
        v = jnp.where(replaced, fresh[:, HW : 2 * HW], v).astype(jnp.bfloat16)
        kdoc[r] = k
        vdoc[r] = v
        pltpu.make_async_copy(kdoc.at[r], ctx_ref.at[0, place(j)], kout.at[r]).start()
        pltpu.make_async_copy(vdoc.at[r], ctx_ref.at[1, place(j)], vout.at[r]).start()
        return k, v

    def absorb(k, v):
        scores = jnp.dot(k, qt_ref[...], preferred_element_type=jnp.float32)
        before = m_ref[...]
        top = jnp.maximum(before, jnp.max(scores, axis=0, keepdims=True))
        terms = jnp.exp2((scores - top) * factor)
        fade = jnp.exp2((before - top) * factor)
        m_ref[...] = top
        l_ref[...] = l_ref[...] * fade + jnp.sum(terms, axis=0, keepdims=True)
        acc_ref[...] = acc_ref[...] * fade + lax.dot_general(
            v,
            terms.astype(jnp.bfloat16),
            (((0,), (0,)), ((), ())),
            preferred_element_type=jnp.float32,
        )

    def pair(n, _):
        k0, v0 = ready(2 * n)
        k1, v1 = ready(2 * n + 1)
        absorb(jnp.concatenate([k0, k1], axis=0), jnp.concatenate([v0, v1], axis=0))
        return 0

    lax.fori_loop(0, count // 2, pair, 0)

    @pl.when(count % 2 == 1)
    def _():
        absorb(*ready(count - 1))

    if not first:
        live = lax.broadcasted_iota(jnp.int32, (1, SPAN), 1) < count_ref[1]
        for n in range(lanes // SPAN):
            h = slice(n * SPAN, (n + 1) * SPAN)
            mixed = jnp.where(live, acc_ref[:, h] / l_ref[:, h], 0.0)
            out_ref[:, n * HW : (n + 1) * HW] = mixed.T.astype(jnp.bfloat16)

    def finish(r, _):
        pltpu.make_async_copy(kdoc.at[0], ctx_ref.at[0, pl.ds(0, SPAN)], kout.at[r]).wait()
        pltpu.make_async_copy(vdoc.at[0], ctx_ref.at[1, pl.ds(0, SPAN)], vout.at[r]).wait()
        return 0

    lax.fori_loop(0, count, finish, 0)
    if first:
        lax.fori_loop(count_ref[0], MAXDOC, finish, 0)


def attend(first, kbufs, vbufs, table, counts, pos, turns, new, qt, state):
    lanes = qt.shape[1]
    context = jax.ShapeDtypeStruct((2, MAXDOC * SPAN, HW), jnp.bfloat16)
    running = [(1, lanes), (1, lanes), (HW, lanes)]
    if first:
        out_shape = (context, *[jax.ShapeDtypeStruct(s, jnp.float32) for s in running])
        out_specs = (HBM, VMEM, VMEM, VMEM)
    else:
        out_shape = (jax.ShapeDtypeStruct((SPAN, lanes // SPAN * HW), jnp.bfloat16), context)
        out_specs = (VMEM, HBM)
    fixed = 6 + len(kbufs) + len(vbufs)
    documents = MAXDOC // 2
    return pl.pallas_call(
        functools.partial(attend_kernel, first, len(kbufs), len(vbufs)),
        out_shape=out_shape,
        in_specs=[SMEM] * 2
        + [VMEM] * 4
        + [KEPT if first else HBM] * (len(kbufs) + len(vbufs))
        + ([] if first else [VMEM] * 3 + [HBM]),
        out_specs=out_specs,
        scratch_shapes=([] if first else [pltpu.VMEM(s, jnp.float32) for s in running])
        + [pltpu.VMEM((MAXDOC, SPAN, HW), jnp.bfloat16)] * 2
        + [pltpu.VMEM((MAXDOC, 16, HW), jnp.bfloat16)] * 2
        + [pltpu.VMEM((SPAN, HW), jnp.bfloat16)]
        + [pltpu.SemaphoreType.DMA((MAXDOC,))] * 6,
        input_output_aliases={} if first else {fixed + 3: 1},
        compiler_params=pltpu.CompilerParams(vmem_limit_bytes=ROOM),
        cost_estimate=pl.CostEstimate(
            flops=4 * lanes * HW * documents * SPAN,
            bytes_accessed=8 * documents * SPAN * HW,
            transcendentals=lanes * documents * SPAN,
        ),
    )(table, counts, pos, turns, new, qt, *kbufs, *vbufs, *state)


def on_device(
    kv_store,
    kv_scale,
    span_home,
    doc_ids,
    doc_count,
    recompute_rows,
    query_len,
    hidden,
    norm_gain,
    w_q,
    w_kv,
):
    tie = lax.optimization_barrier
    me = lax.axis_index("store")
    my_x, my_z = me // NZ, me % NZ

    scale_rows = jnp.transpose(kv_scale[:, :, 0, :], (1, 0, 2)).reshape(2, -1, 1)
    scale_rows = jnp.pad(scale_rows, ((0, 0), (0, 16 - 2 * STORED), (0, 0)))
    own = jnp.concatenate(
        [
            jnp.transpose(kv_store, (1, 0, 2, 3)).reshape(2, STORED * SPAN, HW),
            jnp.broadcast_to(scale_rows, (2, 16, HW)),
        ],
        axis=1,
    ).reshape(2 * BLOCK, HW)

    def keys_of(a):
        return pack([a], [(0, 0, BLOCK)])

    def values_of(a):
        return pack([a], [(0, BLOCK, BLOCK)])

    z1m, z1p = shift(own, 0, 1), shift(own, 0, -1)
    x1m, x1p = shift(own, 1, 0), shift(own, -1, 0)

    doc_list = doc_ids[0]
    doc_total = doc_count[0]
    span_index = jnp.arange(span_home.shape[0], dtype=jnp.int32)
    position = jnp.sum(
        jnp.where(doc_list[:, None] == span_index[None, :], span_home[None, :], 0), axis=1
    )
    owner, slot = position // STORED, position % STORED
    dx = (owner // NZ - my_x) % NX
    dz = (owner % NZ - my_z) % NZ
    one_x = jnp.where(dx == 3, 0, dx)
    one_z = jnp.where(dz == 4, 6, jnp.where(dz > 4, 14 - 2 * dz, 2 * dz - 1))

    def split(block):
        second = (block == 2) | ((block == 1) & (slot == 2))
        row = block * BLOCK + slot * SPAN
        scale = jnp.where(block == 1, CUT, block * BLOCK + STORED * SPAN)
        scale_second = block * BLOCK + STORED * SPAN - CUT
        return (
            second.astype(jnp.int32),
            jnp.where(second, row - CUT, row),
            jnp.where(second, scale_second, scale),
        )

    live = jnp.arange(MAXDOC) < doc_total
    axis_buf = jnp.where(dx == 0, jnp.where(dz == 0, 0, 3 + one_z), jnp.where(dx == 2, 9, 1 + one_x))
    straight = (dx == 0) | (dz == 0)
    late = (dx != 0) & ((dz == 4) | ((dx == 2) & (one_z >= 4)))
    far = one_z >= 4
    row = slot * SPAN
    key_block = jnp.where(far, one_z - 4, one_z)
    piece, cut_row, cut_scale = split(key_block)
    half = (dx == 2) & ~far & (key_block >= 2)
    kb = jnp.where(far, 15 + one_x, jnp.where(half, 13, 10 + one_x))
    kb = jnp.where(straight, jnp.where((dx == 0) & (dz == 4), 14, axis_buf), kb)
    krow = jnp.where(straight, row, (key_block - 2 * half.astype(jnp.int32)) * BLOCK + row)
    ksc = krow - row + STORED * SPAN
    kb = jnp.where(late, jnp.where(dx == 2, 2 + piece, one_x), kb)
    krow = jnp.where(late & (dx == 2), cut_row, krow)
    ksc = jnp.where(late & (dx == 2), cut_scale, ksc)
    piece, cut_row, cut_scale = split(one_x)
    vb = jnp.where(far, 11 + one_z, 10 + one_z)
    vb = jnp.where(straight, jnp.where((dx == 0) & (dz == 4), 14, axis_buf), vb)
    lone = ((dz == 0) & (dx == 2)) | ((dx == 0) & (dz == 4))
    vrow = jnp.where(straight, jnp.where(lone, row, BLOCK + row), one_x * BLOCK + row)
    vsc = vrow - row + STORED * SPAN
    vb = jnp.where(late, jnp.where(dz == 4, 2 + piece, one_z - 4), vb)
    vrow = jnp.where(late & (dz == 4), cut_row, vrow)
    vsc = jnp.where(late & (dz == 4), cut_scale, vsc)
    facts = jnp.stack([jnp.arange(MAXDOC), slot, kb, krow, ksc, vb, vrow, vsc]).astype(jnp.int32)

    def chosen(flag):
        rank = jnp.sum(jnp.where(jnp.tri(MAXDOC, k=-1, dtype=bool) & flag[None, :], 1, 0), axis=1)
        seat = flag[:, None] & (rank[:, None] == jnp.arange(MAXDOC)[None, :])
        return jnp.sum(jnp.where(seat[None], facts[:, :, None], 0), axis=1)

    early_table, late_table = chosen(live & ~late), chosen(live & late)
    early_count = jnp.sum((live & ~late).astype(jnp.int32))
    counts = jnp.stack([doc_total, query_len[0], early_count, doc_total - early_count]).astype(
        jnp.int32
    )

    shift_cos, shift_sin = rope_angles(jnp.arange(MAXDOC, dtype=jnp.int32) * SPAN, HW)
    turns = jnp.stack(
        [
            jnp.concatenate([shift_cos, shift_cos], axis=1),
            jnp.concatenate([-shift_sin, shift_sin], axis=1),
        ],
        axis=1,
    )

    recompute_total = recompute_rows.shape[1] * recompute_rows.shape[2]
    flat_pos = recompute_rows[0].reshape(recompute_total).astype(jnp.int32)
    query_pos = doc_total * SPAN + jnp.arange(hidden.shape[1] - recompute_total, dtype=jnp.int32)
    row_cos, row_sin = rope_angles(jnp.concatenate([flat_pos, query_pos]), HW)
    layer_input = lax.all_gather(hidden, "tp", axis=2, tiled=True)[0]
    small = (
        norm_gain[None],
        w_kv.reshape(w_kv.shape[0], 2 * HW),
        jnp.concatenate([row_cos, row_sin], axis=1),
        early_table,
        late_table,
        counts,
        flat_pos[None],
        turns,
    )
    z1m, z1p, x1m, x1p, small = tie((z1m, z1p, x1m, x1p, small))
    gain, w_kv, angles, early_table, late_table, counts, pos, turns = small

    z2m, z2p = shift(z1m, 0, 1), shift(z1p, 0, -1)
    x2v = shift(values_of(x1p), -1, 0)
    w0 = pack([x1m, x1p, x2v], [(0, BLOCK, BLOCK), (1, BLOCK, BLOCK), (2, 0, BLOCK)])
    w1m, w1p = shift(w0, 0, 1), shift(w0, 0, -1)
    z3m, z3p = shift(z2m, 0, 1), shift(z2p, 0, -1)
    d1 = pack([z1m, z1p, z2m, z2p], [(n, 0, BLOCK) for n in range(4)])
    d1m, d1p = shift(d1, 1, 0), shift(d1, -1, 0)
    w2m, w2p = shift(w1m, 0, 1), shift(w1p, 0, -1)
    z4k = shift(keys_of(z3m), 0, 1)
    d2 = pack([z3m, z3p, z4k], [(n, 0, BLOCK) for n in range(3)])
    d2m, d2p = shift(d2, 1, 0), shift(d2, -1, 0)
    w3m, w3p = shift(w2m, 0, 1), shift(w2p, 0, -1)
    layer_input, _, _ = tie((layer_input, w2m, z4k))
    new, qt = project(layer_input, gain, w_q, w_kv, angles)
    x1k, z3v, d1m, d1p, new, qt = tie((x1m, z3p, d1m, d1p, new, qt))
    d1a = shift(pack([d1m], [(0, 0, 2 * BLOCK)]), 1, 0)
    x2k = shift(keys_of(x1k), 1, 0)
    z4v = shift(values_of(z3v), 0, -1)
    d1b = shift(pack([d1p], [(0, 2 * BLOCK, 2 * BLOCK)]), -1, 0)
    w3m, w3p, d2m, d2p, new, qt = tie((w3m, w3p, d2m, d2p, new, qt))
    w_left, w_right, d_left, d_right = halves(w3m, w3p, d2m, d2p)
    w4a, w4b = shift(w_left, 0, 1), shift(w_right, 0, -1)
    d2a, d2b = shift(d_left, 1, 0), shift(d_right, -1, 0)
    straight_bufs = [own, x1m, x1p, z1m, z1p, z2m, z2p, z3m, z3p]
    common = (counts, pos, turns, new, qt)
    context, *state = attend(
        True,
        straight_bufs + [x2k, d1m, d1p, d1a, d1b, z4k, d2m, d2p],
        straight_bufs + [x2v, w1m, w1p, w2m, w2p, z4v, w3m, w3p],
        early_table,
        *common,
        [],
    )
    attention, context = attend(
        False,
        [d2m, d2p, d2a, d2b],
        [w3m, w3p, w4a, w4b],
        late_table,
        *common,
        [*state, context],
    )
    return (attention[None], context[None])


def solution(mesh):
    placed = (
        P("store", None, None, "tp"),
        P("store", None, "tp", None),
        P(),
        P("store", None),
        P("store"),
        P("store", None, None),
        P("store"),
        P("store", None, "tp"),
        P(),
        P(None, "tp"),
        P(None, None, "tp"),
    )
    return jax.shard_map(
        on_device,
        mesh=mesh,
        in_specs=placed,
        out_specs=(P("store", None, "tp"), P("store", None, None, "tp")),
        check_vma=False,
    )
```
